32 devices in a mesh: seq: 4 (over y, x), dp: 8 (over z, core).
Axes of the slice: x: 2, y: 2, z: 4, core: 2. Of those that a mesh axis runs over, the one named last changes fastest.
Arguments:
- frames_in: bfloat16 [8, 4, 8, 320, 128], P('dp', 'seq'), may hold values from -6 to 6
- spatial_kernel: bfloat16 [9, 320, 320], P(None, 'seq'), may hold values from -0.109375 to 0.109375
- temporal_kernel: bfloat16 [3, 320, 320], P(None, 'seq'), may hold values from -0.1875 to 0.1875
- out_cotangent: bfloat16 [8, 4, 8, 320, 128], P('dp', 'seq'), may hold values from -6 to 6
Outputs:
- block_out: bfloat16 [8, 4, 8, 320, 128], P('dp', 'seq')
- input_grad: bfloat16 [8, 4, 8, 320, 128], P('dp', 'seq')
- spatial_grad: float32 [9, 320, 320], P(None, 'seq')
- temporal_grad: float32 [3, 320, 320], P(None, 'seq')
The draws below stay inside these ranges and needn't reach their ends.
All inputs are finite; a program needn't handle non-finite values.
Results may differ from the reference program's by a relative error of at most 0.0055.
Values may be sent and summed in bfloat16 or wider, within the bound.
No kernel may reach another device: no remote copies, remote signals or barrier semaphores. Data moves between devices by JAX's collectives and lax.ppermute only.
A program may use at most 128 MiB of HBM per device.

```python
import math
import jax
import jax.numpy as jnp
from jax import lax

C = 320
WIDTH = 128
FRAMES = 4
HEIGHT = 8
CLIPS = 8


def raised(result, rng, source, target, blocks, factor):
    owner, partner = [(jnp.arange(result.shape[axis_at]) // (result.shape[axis_at] // blocks)).reshape([-1 if axis == axis_at else 1 for axis in range(result.ndim)]) for axis_at in (source, target)]
    chosen = jax.random.permutation(rng, blocks)[partner]
    strong = (owner == chosen) | (owner == (partner + blocks // 2) % blocks)
    return jnp.where(strong, factor * result, result)


def block_levels(stream_key, dims, cuts, smallest, top_value):
    factor_of = 1.0
    for position, parts in cuts:
        heights = jax.random.uniform(jax.random.fold_in(jax.random.fold_in(stream_key, 6), position), (parts,), jnp.float32, smallest / len(cuts), top_value / len(cuts))
        factor_of = factor_of * jnp.repeat(jnp.exp(heights), dims[position] // parts).reshape((-1,) + (1,) * (len(dims) - 1 - position))
    return factor_of


def bell_draw(rng, shape, deviation, limit, cuts=(), dtype=jnp.bfloat16):
    array = deviation * jax.random.normal(rng, shape, jnp.float32)
    if cuts:
        array = array * block_levels(rng, shape, cuts, -0.22, 0.18)
    return jnp.clip(array, -limit, limit).astype(dtype)


def bell_draw_with(rng, extent, scale, reach, shards, heavy, held_as=jnp.bfloat16):
    drawn = scale * jax.random.normal(rng, extent, jnp.float32)
    if shards:
        drawn = drawn * block_levels(rng, extent, shards, -0.22, 0.18)
    return jnp.clip(raised(drawn, jax.random.fold_in(rng, 3), *heavy), -reach, reach).astype(held_as)


def setup_inputs(seed: int = 0) -> dict:
    keys = jax.random.split(jax.random.key(seed), 5)
    return {
        "frames_in": bell_draw(keys[0], (CLIPS, FRAMES, HEIGHT, C, WIDTH), 1.0, 6.0, ((0, 8), (1, 4))),
        "spatial_kernel": bell_draw(keys[1], (9, C, C), (9 * C) ** -0.5, 0.109375, ((1, 4),)),
        "temporal_kernel": bell_draw(keys[2], (3, C, C), (3 * C) ** -0.5, 0.1875, ((1, 4),)),
        "out_cotangent": bell_draw_with(keys[3], (CLIPS, FRAMES, HEIGHT, C, WIDTH), 1.0, 6.0, ((0, 8), (1, 4)), (1, 3, 4, 2.0)),
    }


def pad_frames(values):
    return jnp.pad(values, ((0, 0), (1, 1), (0, 0), (0, 0), (0, 0)))

def pad_pixels(values):
    return jnp.pad(values, ((0, 0), (0, 0), (1, 1), (0, 0), (1, 1)))

def spatial_forward(frames, kernel):
    row_count = frames.shape[2]
    col_count = frames.shape[4]
    padded = pad_pixels(frames).astype(jnp.float32)
    kernel_wide = kernel.astype(jnp.float32)
    running = jnp.zeros(frames.shape[:3] + (kernel.shape[1], col_count), jnp.float32)
    for offset_row in range(3):
        for offset_col in range(3):
            window = padded[:, :, offset_row:offset_row + row_count, :, offset_col:offset_col + col_count]
            running = running + jnp.einsum('oc,bfhcw->bfhow', kernel_wide[3 * offset_row + offset_col], window)
    return running

def spatial_backward(pre_grad, kernel):
    row_count = pre_grad.shape[2]
    col_count = pre_grad.shape[4]
    padded = pad_pixels(pre_grad).astype(jnp.float32)
    kernel_wide = kernel.astype(jnp.float32)
    running = jnp.zeros(pre_grad.shape[:3] + (kernel.shape[2], col_count), jnp.float32)
    for offset_row in range(3):
        for offset_col in range(3):
            window = padded[:, :, 2 - offset_row:2 - offset_row + row_count, :, 2 - offset_col:2 - offset_col + col_count]
            running = running + jnp.einsum('oc,bfhow->bfhcw', kernel_wide[3 * offset_row + offset_col], window)
    return running

def spatial_weight_grad(frames, pre_grad):
    row_count = frames.shape[2]
    col_count = frames.shape[4]
    padded = pad_pixels(frames).astype(jnp.float32)
    grad_wide = pre_grad.astype(jnp.float32)
    pieces = []
    for offset_row in range(3):
        for offset_col in range(3):
            window = padded[:, :, offset_row:offset_row + row_count, :, offset_col:offset_col + col_count]
            pieces.append(jnp.einsum('bfhow,bfhcw->oc', grad_wide, window))
    return jnp.stack(pieces)

def temporal_forward(padded_act, kernel):
    frame_count = padded_act.shape[1] - 2
    padded = padded_act.astype(jnp.float32)
    kernel_wide = kernel.astype(jnp.float32)
    running = jnp.zeros(padded.shape[:1] + (frame_count,) + padded.shape[2:3] + (kernel.shape[1], padded.shape[4]), jnp.float32)
    for offset in range(3):
        running = running + jnp.einsum('oc,bfhcw->bfhow', kernel_wide[offset], padded[:, offset:offset + frame_count])
    return running

def temporal_backward(padded_cot, kernel):
    frame_count = padded_cot.shape[1] - 2
    padded = padded_cot.astype(jnp.float32)
    kernel_wide = kernel.astype(jnp.float32)
    running = jnp.zeros(padded.shape[:1] + (frame_count,) + padded.shape[2:3] + (kernel.shape[2], padded.shape[4]), jnp.float32)
    for offset in range(3):
        running = running + jnp.einsum('oc,bfhow->bfhcw', kernel_wide[offset], padded[:, 2 - offset:2 - offset + frame_count])
    return running

def temporal_weight_grad(cotangent, padded_act):
    frame_count = cotangent.shape[1]
    cot_wide = cotangent.astype(jnp.float32)
    padded = padded_act.astype(jnp.float32)
    pieces = []
    for offset in range(3):
        pieces.append(jnp.einsum('bfhow,bfhcw->oc', cot_wide, padded[:, offset:offset + frame_count]))
    return jnp.stack(pieces)

def clip_pass(frames, cotangent, spatial_kernel, temporal_kernel):
    frames = frames[None]
    cotangent = cotangent[None]
    pre_act = lax.optimization_barrier(spatial_forward(frames, spatial_kernel).astype(jnp.bfloat16))
    pre_wide = pre_act.astype(jnp.float32)
    activated = jax.nn.silu(pre_wide).astype(jnp.bfloat16)
    padded_act = pad_frames(activated)
    temporal = lax.optimization_barrier(temporal_forward(padded_act, temporal_kernel).astype(jnp.bfloat16))
    block_out = (frames.astype(jnp.float32) + temporal.astype(jnp.float32)).astype(jnp.bfloat16)
    act_grad = lax.optimization_barrier(temporal_backward(pad_frames(cotangent), temporal_kernel).astype(jnp.bfloat16))
    temporal_part = temporal_weight_grad(cotangent, padded_act)
    sigmoid_value = jax.nn.sigmoid(pre_wide)
    pre_grad = (act_grad.astype(jnp.float32) * sigmoid_value * (1.0 + pre_wide * (1.0 - sigmoid_value))).astype(jnp.bfloat16)
    spatial_part = spatial_weight_grad(frames, pre_grad)
    input_grad = (cotangent.astype(jnp.float32) + spatial_backward(pre_grad, spatial_kernel)).astype(jnp.bfloat16)
    return (block_out[0], input_grad[0], spatial_part, temporal_part)

def reference(frames_in, spatial_kernel, temporal_kernel, out_cotangent):

    def one_clip(clip_pair):
        return clip_pass(clip_pair[0], clip_pair[1], spatial_kernel, temporal_kernel)
    results = lax.map(one_clip, (frames_in, out_cotangent))
    grad_scale = 1.0 / math.sqrt(CLIPS * FRAMES * HEIGHT * WIDTH)
    spatial_grad = lax.optimization_barrier(jnp.sum(results[2], axis=0)) * grad_scale
    temporal_grad = lax.optimization_barrier(jnp.sum(results[3], axis=0)) * grad_scale
    return (results[0], results[1], spatial_grad, temporal_grad)
```

```python
import functools
import math

import jax
import jax.numpy as jnp
from jax import lax
from jax.experimental import pallas as pl
from jax.experimental.pallas import tpu as pltpu
from jax.sharding import PartitionSpec as P

BF = jnp.bfloat16
F32 = jnp.float32
VMEM_LIMIT = 56 * 1024 * 1024


def call(body, outs, scratch, flops, moved, *args):
    return pl.pallas_call(
        body,
        out_shape=outs,
        in_specs=[pl.BlockSpec(memory_space=pltpu.VMEM)] * len(args),
        out_specs=jax.tree.map(lambda _: pl.BlockSpec(memory_space=pltpu.VMEM), outs),
        scratch_shapes=scratch,
        compiler_params=pltpu.CompilerParams(vmem_limit_bytes=VMEM_LIMIT),
        cost_estimate=pl.CostEstimate(flops=flops, bytes_accessed=moved, transcendentals=0),
    )(*args)


def shape(dims, dtype=BF):
    return jax.ShapeDtypeStruct(tuple(dims), dtype)


def columns_of(first, count, width):
    return pl.ds(pl.multiple_of(first * width, width), count * width)


def shifted(block, step):
    if step == 0:
        return block
    width = block.shape[1]
    wide = block.astype(F32)
    rolled = pltpu.roll(wide, (-step) % width, 1)
    column = lax.broadcasted_iota(jnp.int32, block.shape, 1)
    edge = 0 if step < 0 else width - 1
    return jnp.where(column == edge, 0.0, rolled).astype(block.dtype)


def fill_taps(target, source, order):
    rows, chans, width = source.shape
    target[:, :width] = jnp.zeros((target.shape[0], width), target.dtype)
    target[:, (rows + 1) * width :] = jnp.zeros((target.shape[0], width), target.dtype)

    def row(y, carry):
        block = source[y]
        for b, step in enumerate(order):
            target[b * chans : (b + 1) * chans, columns_of(y + 1, 1, width)] = shifted(block, step)
        return carry

    lax.fori_loop(0, rows, row, 0)


def place_taps(target, tap, pieces, shard):
    me = lax.axis_index("seq")
    for j, piece in enumerate(pieces):
        at = pl.multiple_of(jnp.bitwise_xor(me, j) * shard, shard)
        target[tap, pl.ds(at, shard), :] = piece


def spatial_forward(frames, weights):
    rows, chans, width = frames.shape

    def body(frames_ref, weights_ref, pre_ref, act_ref, taps_ref):
        fill_taps(taps_ref, frames_ref, (-1, 0, 1))

        def tile(i, carry):
            total = jnp.zeros((chans, 2 * width), F32)
            for a in range(3):
                total += jnp.dot(
                    weights_ref[a],
                    taps_ref[:, columns_of(2 * i + a, 2, width)],
                    preferred_element_type=F32,
                )
            pre = total.astype(BF)
            wide = pre.astype(F32)
            act = (wide / (1.0 + jnp.exp(-wide))).astype(BF)
            for r in range(2):
                pre_ref[2 * i + r] = pre[:, r * width : (r + 1) * width]
                act_ref[2 * i + r] = act[:, r * width : (r + 1) * width]
            return carry

        lax.fori_loop(0, rows // 2, tile, 0)

    return call(
        body,
        (shape(frames.shape), shape(frames.shape)),
        [pltpu.VMEM((3 * chans, (rows + 2) * width), BF)],
        18 * chans * chans * rows * width,
        6 * frames.size + 18 * chans * chans,
        frames,
        weights,
    )


def spatial_weight_grad(frames, pre_act, act_grad, scale):
    rows, chans, width = frames.shape

    def body(frames_ref, pre_ref, grad_ref, pg_ref, out_ref, taps_ref, flat_ref):
        fill_taps(taps_ref, frames_ref, (-1, 0, 1))

        def row(y, carry):
            wide = pre_ref[y].astype(F32)
            s = 1.0 / (1.0 + jnp.exp(-wide))
            pg = (grad_ref[y].astype(F32) * s * (1.0 + wide * (1.0 - s))).astype(BF)
            pg_ref[y] = pg
            flat_ref[:, columns_of(y, 1, width)] = pg
            return carry

        lax.fori_loop(0, rows, row, 0)
        for a in range(3):
            out_ref[a] = (
                lax.dot_general(
                    flat_ref[...],
                    taps_ref[:, a * width : (a + rows) * width],
                    (((1,), (1,)), ((), ())),
                    preferred_element_type=F32,
                )
                * scale
            ).astype(out_ref.dtype)

    return call(
        body,
        (shape(frames.shape), shape((3, chans, 3 * chans), F32)),
        [
            pltpu.VMEM((3 * chans, (rows + 2) * width), BF),
            pltpu.VMEM((chans, rows * width), BF),
        ],
        18 * chans * chans * rows * width,
        8 * frames.size + 36 * chans * chans,
        frames,
        pre_act,
        act_grad,
    )


def spatial_backward(pre_grad, cotangent, weights_t):
    rows, chans, width = pre_grad.shape

    def body(pg_ref, cot_ref, weights_ref, out_ref, taps_ref):
        fill_taps(taps_ref, pg_ref, (1, 0, -1))

        def tile(i, carry):
            total = jnp.zeros((chans, 2 * width), F32)
            for a in range(3):
                total += jnp.dot(
                    weights_ref[a],
                    taps_ref[:, columns_of(2 * i + 2 - a, 2, width)],
                    preferred_element_type=F32,
                )
            for r in range(2):
                wide = cot_ref[2 * i + r].astype(F32)
                out_ref[2 * i + r] = (wide + total[:, r * width : (r + 1) * width]).astype(BF)
            return carry

        lax.fori_loop(0, rows // 2, tile, 0)

    return call(
        body,
        shape(pre_grad.shape),
        [pltpu.VMEM((3 * chans, (rows + 2) * width), BF)],
        18 * chans * chans * rows * width,
        6 * pre_grad.size + 18 * chans * chans,
        pre_grad,
        cotangent,
        weights_t,
    )


def temporal_apply(values, weights, forward):
    frames, rows, chans, width = values.shape
    span = rows * width

    def body(values_ref, weights_ref, out_ref, taps_ref):
        taps_ref[...] = jnp.zeros(taps_ref.shape, BF)
        for k in range(3):
            step = k - 1 if forward else 1 - k
            for f in range(frames):
                if 0 <= f - step < frames:
                    for y in range(rows):
                        at = (f - step) * span + y * width
                        taps_ref[k * chans : (k + 1) * chans, at : at + width] = values_ref[f, y]
        for f in range(frames):
            total = jnp.dot(
                weights_ref[...],
                taps_ref[:, f * span : (f + 1) * span],
                preferred_element_type=F32,
            ).astype(BF)
            for y in range(rows):
                out_ref[f, y] = total[:, y * width : (y + 1) * width]

    return call(
        body,
        shape(values.shape),
        [pltpu.VMEM((3 * chans, frames * span), BF)],
        6 * chans * values.size,
        4 * values.size + 6 * chans * chans,
        values,
        weights,
    )


def temporal_weight_grad(cotangent, activated, scale):
    frames, rows, chans, width = activated.shape
    span = rows * width

    def body(cot_ref, act_ref, out_ref, cot_flat, taps_ref):
        taps_ref[...] = jnp.zeros(taps_ref.shape, BF)
        for f in range(frames):
            for y in range(rows):
                at = f * span + y * width
                cot_flat[:, at : at + width] = cot_ref[f, y]
                for k in range(3):
                    if 0 <= f - k + 1 < frames:
                        to = at + (1 - k) * span
                        taps_ref[k * chans : (k + 1) * chans, to : to + width] = act_ref[f, y]
        out_ref[...] = (
            lax.dot_general(
                cot_flat[...],
                taps_ref[...],
                (((1,), (1,)), ((), ())),
                preferred_element_type=F32,
            )
            * scale
        ).astype(out_ref.dtype)

    return call(
        body,
        shape((chans, 3 * chans), F32),
        [
            pltpu.VMEM((chans, frames * span), BF),
            pltpu.VMEM((3 * chans, frames * span), BF),
        ],
        6 * chans * activated.size,
        4 * activated.size + 12 * chans * chans,
        cotangent,
        activated,
    )


def swap(values, axis, bit):
    size = lax.axis_size(axis)
    return lax.ppermute(values, axis, [(i, i ^ bit) for i in range(size)])


def gather_taps(shards):
    size = lax.axis_size("seq")
    taps, shard, chans = shards.shape
    half = taps // 2
    core = lax.axis_index("dp") % 2
    mine = lax.dynamic_slice_in_dim(shards, core * half, half, 0)
    got = jnp.stack([swap(mine, "seq", j) for j in range(1, size)])
    other = swap(got, "dp", 1)
    low = jnp.where(core == 0, got, other)
    high = jnp.where(core == 0, other, got)
    return jnp.concatenate([shards[None], jnp.concatenate([low, high], axis=1)])


def ordered(pieces):
    size, taps, shard, chans = pieces.shape
    me = lax.axis_index("seq")
    full = jnp.zeros((taps, size * shard, chans), pieces.dtype)
    for j in range(size):
        full = lax.dynamic_update_slice_in_dim(full, pieces[j], (me ^ j) * shard, 1)
    return full


def reduce_half(values, axis, bit, dim):
    mine = lax.axis_index(axis) // bit % 2
    kept = lax.dynamic_index_in_dim(values, mine, dim, keepdims=False)
    sent = lax.dynamic_index_in_dim(values, 1 - mine, dim, keepdims=False)
    return kept + swap(sent.astype(BF), axis, bit).astype(F32)


def join_half(values, axis, bit, dim):
    mine = lax.axis_index(axis) // bit % 2
    other = swap(values, axis, bit)
    return jnp.stack(
        [jnp.where(mine == 0, values, other), jnp.where(mine == 0, other, values)], dim
    )


def reduce_kernels(partial):
    seq = lax.axis_size("seq")
    dp = lax.axis_size("dp")
    groups, chans, width = partial.shape
    values = reduce_half(partial.reshape(2, groups // 2, chans, width), "dp", 1, 0)
    bits = [1 << i for i in range(seq.bit_length() - 1)]
    done = []
    for g in range(groups // 2):
        order = bits if g % 2 == 0 else bits[::-1]
        part = values[g].reshape([2] * len(bits) + [chans // seq, width])
        left = bits[::-1]
        for bit in order:
            at = left.index(bit)
            part = reduce_half(part, "seq", bit, at)
            left = [b for b in left if b != bit]
        done.append(part)
    part = jnp.stack(done)
    part = part.reshape((2, groups // 4) + part.shape[1:])
    part = reduce_half(part, "dp", 2, 0)
    bit = 4
    while bit < dp:
        part = part.astype(BF).astype(F32) + swap(part.astype(BF), "dp", bit).astype(F32)
        bit *= 2
    part = part.astype(BF)
    part = join_half(part, "dp", 2, 0).reshape((groups // 2,) + part.shape[1:])
    part = join_half(part, "dp", 1, 0).reshape((groups,) + part.shape[1:])
    return part


def local(frames_in, spatial_kernel, temporal_kernel, out_cotangent):
    frames, cotangent = frames_in[0, 0], out_cotangent[0, 0]
    rows, chans, width = frames.shape
    seq = lax.axis_size("seq")
    shard = spatial_kernel.shape[1]
    scale = 1.0 / math.sqrt(lax.axis_size("dp") * seq * rows * width)

    cot_rows = lax.all_to_all(
        cotangent.reshape(seq, rows // seq, chans, width), "seq", 0, 0, tiled=True
    )
    kernels = ordered(gather_taps(jnp.concatenate([temporal_kernel, spatial_kernel])))
    temporal_t = kernels[:3].transpose(2, 0, 1).reshape(chans, 3 * chans)
    temporal_w = kernels[:3].transpose(1, 0, 2).reshape(chans, 3 * chans)
    spatial = kernels[3:].reshape(3, 3, chans, chans)
    spatial_w = spatial.transpose(0, 2, 1, 3).reshape(3, chans, 3 * chans)
    spatial_t = spatial.transpose(0, 3, 1, 2).reshape(3, chans, 3 * chans)

    grad_rows = temporal_apply(cot_rows, temporal_t, False)
    act_grad = lax.all_to_all(grad_rows, "seq", 0, 0, tiled=True).reshape(frames.shape)
    pre_act, activated = spatial_forward(frames, spatial_w)
    act_rows = lax.all_to_all(
        activated.reshape(seq, rows // seq, chans, width), "seq", 0, 0, tiled=True
    )
    temporal_rows = temporal_apply(act_rows, temporal_w, True)
    temporal = lax.all_to_all(temporal_rows, "seq", 0, 0, tiled=True).reshape(frames.shape)
    temporal_part = temporal_weight_grad(cot_rows, act_rows, scale)
    pre_grad, spatial_part = spatial_weight_grad(frames, pre_act, act_grad, scale)
    input_grad = spatial_backward(pre_grad, cotangent, spatial_t)
    block_out = (frames.astype(F32) + temporal.astype(F32)).astype(BF)
    total = reduce_kernels(jnp.concatenate([spatial_part, temporal_part[None]])).astype(F32)
    total = total.reshape(4, shard, 3, chans).transpose(0, 2, 1, 3).reshape(12, shard, chans)
    return (block_out[None, None], input_grad[None, None], total[:9], total[9:])


def solution(mesh):
    placed = (
        P("dp", "seq", None, None, None),
        P(None, "seq", None),
        P(None, "seq", None),
        P("dp", "seq", None, None, None),
    )
    return jax.shard_map(
        local,
        mesh=mesh,
        in_specs=placed,
        out_specs=(
            P("dp", "seq", None, None, None),
            P("dp", "seq", None, None, None),
            P(None, "seq", None),
            P(None, "seq", None),
        ),
        check_vma=False,
    )
```

```python
import math

import jax
import jax.numpy as jnp
from jax import lax
from jax.experimental import pallas as pl
from jax.experimental.pallas import tpu as pltpu
from jax.sharding import PartitionSpec as P

BF = jnp.bfloat16
F32 = jnp.float32
VMEM_LIMIT = 24 * 1024 * 1024
NT = (((1,), (1,)), ((), ()))


def call(body, outs, scratch, flops, *args):
    moved = sum(x.size * x.dtype.itemsize for x in (*args, *outs))
    return pl.pallas_call(
        body,
        out_shape=tuple(outs),
        in_specs=[pl.BlockSpec(memory_space=pltpu.VMEM)] * len(args),
        out_specs=tuple(pl.BlockSpec(memory_space=pltpu.VMEM) for _ in outs),
        scratch_shapes=scratch,
        compiler_params=pltpu.CompilerParams(vmem_limit_bytes=VMEM_LIMIT),
        cost_estimate=pl.CostEstimate(flops=flops, bytes_accessed=moved, transcendentals=0),
    )(*args)


def shape(dims, dtype=BF):
    return jax.ShapeDtypeStruct(tuple(dims), dtype)


def columns(first, count, width):
    return pl.ds(pl.multiple_of(first * width, width), count * width)


def place(step):
    return jnp.bitwise_xor(lax.axis_index("seq"), step)


def core():
    return lax.rem(lax.axis_index("dp"), 2)


def pair_bit():
    return lax.rem(lax.div(lax.axis_index("dp"), 2), 2)


def at_block(index, size, count, tile, use):
    if size % tile == 0:
        use(pl.ds(pl.multiple_of(index * size, size), size))
        return
    for fixed in range(count):

        @pl.when(index == fixed)
        def _():
            use(pl.ds(fixed * size, size))


def swap(values, axis, bit):
    size = lax.axis_size(axis)
    return lax.ppermute(values, axis, [(i, i ^ bit) for i in range(size)])


def spread(blocks):
    return [swap(block, "seq", j + 1) for j, block in enumerate(blocks)]


def after(value, *others):
    return lax.optimization_barrier((value, *others))[0]


def shifted(block, step):
    if step == 0:
        return block
    width = block.shape[1]
    rolled = pltpu.roll(block.astype(F32), (-step) % width, 1)
    column = lax.broadcasted_iota(jnp.int32, block.shape, 1)
    edge = 0 if step < 0 else width - 1
    return jnp.where(column == edge, 0.0, rolled).astype(block.dtype)


def fill_taps(target, source, order):
    rows, chans, width = source.shape
    target[:, :width] = jnp.zeros((target.shape[0], width), target.dtype)
    target[:, (rows + 1) * width :] = jnp.zeros((target.shape[0], width), target.dtype)

    def row(y, carry):
        block = source[y]
        for b, step in enumerate(order):
            target[b * chans : (b + 1) * chans, columns(y + 1, 1, width)] = shifted(block, step)
        return carry

    lax.fori_loop(0, rows, row, 0)


def transposed(block):
    size = block.shape[0]
    one = lax.broadcasted_iota(jnp.int32, (size, size), 0) == lax.broadcasted_iota(
        jnp.int32, (size, size), 1
    )
    return lax.dot_general(one.astype(BF), block, NT, preferred_element_type=F32).astype(BF)


def window_taps(frames):
    rows, chans, width = frames.shape
    return call(
        lambda source, target: fill_taps(target, source, (-1, 0, 1)),
        [shape((3 * chans, (rows + 2) * width))],
        [],
        frames.size,
        frames,
    )[0]


def temporal_maps(own, first, second):
    _, shard, chans = own.shape
    count = len(first)

    def body(*refs):
        own_ref = refs[0]
        mine, theirs = refs[1 : 1 + count], refs[1 + count : 1 + 2 * count]
        plain_ref, trans_ref, rows_ref = refs[1 + 2 * count :]

        def fill(pieces):
            for j, piece in enumerate((own_ref, *pieces)):

                def put(at):
                    for k in range(3):
                        rows_ref[k, at, :] = piece[k]

                at_block(place(j), shard, count + 1, 16, put)

        @pl.when(core() == 0)
        def _():
            fill(mine)

        @pl.when(core() == 1)
        def _():
            fill(theirs)

        for k in range(3):
            plain_ref[:, k * chans : (k + 1) * chans] = rows_ref[k]
            trans_ref[:, k * chans : (k + 1) * chans] = transposed(rows_ref[k])

    return call(
        body,
        [shape((chans, 3 * chans))] * 2,
        [pltpu.VMEM((3, chans, chans), BF)],
        6 * chans**3,
        own,
        *first,
        *second,
    )


def temporal_backward(cot_rows, weights_t):
    frames, rows, chans, width = cot_rows.shape
    span = rows * width

    def body(cot_ref, weights_ref, *refs):
        outs, taps_ref = refs[:frames], refs[frames]
        edge = jnp.zeros((chans, span), BF)
        taps_ref[:chans, (frames - 1) * span :] = edge
        taps_ref[2 * chans :, :span] = edge
        for f in range(frames):
            for k in range(3):
                at = f + k - 1
                if 0 <= at < frames:
                    for y in range(rows):
                        to = at * span + y * width
                        taps_ref[k * chans : (k + 1) * chans, to : to + width] = cot_ref[f, y]
        for j in range(frames):
            total = jnp.dot(
                weights_ref[...],
                taps_ref[:, columns(place(j), 1, span)],
                preferred_element_type=F32,
            ).astype(BF)
            for y in range(rows):
                outs[j][y] = total[:, y * width : (y + 1) * width]

    return call(
        body,
        [shape((rows, chans, width))] * frames,
        [pltpu.VMEM((3 * chans, frames * span), BF)],
        6 * chans * cot_rows.size,
        cot_rows,
        weights_t,
    )


def spatial_forward(taps, own, first_a, second_a, first_b, second_b, rows):
    _, shard, chans = own.shape
    count = len(first_a)
    width = taps.shape[1] // (rows + 2)
    block = rows // (count + 1)

    def body(*refs):
        taps_ref, own_ref = refs[:2]
        lists = [refs[2 + i * count : 2 + (i + 1) * count] for i in range(4)]
        refs = refs[2 + 4 * count :]
        pre_ref, weights_ref, outs, act_ref = refs[0], refs[1], refs[2:-1], refs[-1]

        def fill(row, pieces, first_tap):
            for j, piece in enumerate((own_ref, *pieces)):

                def put(at):
                    for b in range(3):
                        source = piece[first_tap + b] if j == 0 else piece[b]
                        weights_ref[row, at, b * chans : (b + 1) * chans] = source

                at_block(place(j), shard, count + 1, 16, put)

        @pl.when(core() == 0)
        def _():
            fill(0, lists[2], 0)
            fill(1, lists[1], 3)
            fill(2, lists[3], 6)

        @pl.when(core() == 1)
        def _():
            fill(0, lists[3], 0)
            fill(1, lists[0], 3)
            fill(2, lists[2], 6)

        def tile(i, carry):
            total = jnp.zeros((chans, 2 * width), F32)
            for a in range(3):
                total += jnp.dot(
                    weights_ref[a],
                    taps_ref[:, columns(2 * i + a, 2, width)],
                    preferred_element_type=F32,
                )
            pre = total.astype(BF)
            wide = pre.astype(F32)
            act = (wide / (1.0 + jnp.exp(-wide))).astype(BF)
            for r in range(2):
                pre_ref[2 * i + r] = pre[:, r * width : (r + 1) * width]
                act_ref[2 * i + r] = act[:, r * width : (r + 1) * width]
            return carry

        lax.fori_loop(0, rows // 2, tile, 0)
        for j, out in enumerate(outs):
            out[...] = act_ref[pl.ds(place(j) * block, block)]

    pre, weights, *acts = call(
        body,
        [shape((rows, chans, width)), shape((3, chans, 3 * chans))]
        + [shape((block, chans, width))] * (count + 1),
        [pltpu.VMEM((rows, chans, width), BF)],
        18 * chans * chans * rows * width,
        taps,
        own,
        *first_a,
        *second_a,
        *first_b,
        *second_b,
    )
    return pre, weights, acts


def activation_grad(pre_act, grads, shard):
    rows, chans, width = pre_act.shape
    block = rows // len(grads)
    half = shard // 2

    def body(*refs):
        pre_ref, grad_refs = refs[0], refs[1 : 1 + len(grads)]
        pg_ref, mine_ref, theirs_ref, act_ref = refs[1 + len(grads) :]
        for j, ref in enumerate(grad_refs):
            act_ref[pl.ds(place(j) * block, block)] = ref[...]

        def row(y, carry):
            wide = pre_ref[y].astype(F32)
            s = 1.0 / (1.0 + jnp.exp(-wide))
            pg = act_ref[y].astype(F32) * s * (1.0 + wide * (1.0 - s))
            pg_ref[y] = pg.astype(BF)
            low = [pg[at : at + half] for at in range(0, chans, shard)]
            high = [pg[at + half : at + shard] for at in range(0, chans, shard)]
            low = jnp.concatenate(low).astype(BF)
            high = jnp.concatenate(high).astype(BF)
            first = core() == 0
            mine_ref[:, columns(y, 1, width)] = jnp.where(first, low, high)
            theirs_ref[:, columns(y, 1, width)] = jnp.where(first, high, low)
            return carry

        lax.fori_loop(0, rows, row, 0)

    return call(
        body,
        [shape(pre_act.shape)] + [shape((chans // 2, rows * width))] * 2,
        [pltpu.VMEM(pre_act.shape, BF)],
        20 * pre_act.size,
        pre_act,
        *grads,
    )


def spatial_weight_grad(taps, other_taps, half_grad, other_half, owners, scale, width):
    wide = taps.shape[0]
    chans, span = half_grad.shape
    part = chans // owners

    def body(taps_ref, other_ref, mine_ref, theirs_ref, *refs):
        keep_ref, sends, stack_ref, total_ref = refs[0], refs[1:-2], refs[-2], refs[-1]
        edge = jnp.zeros((chans, width), BF)
        for q, source in enumerate((mine_ref, theirs_ref)):
            at = q * span
            stack_ref[:chans, at + span - width : at + span] = edge
            stack_ref[:chans, at : at + span - width] = source[:, width:]
            stack_ref[chans : 2 * chans, at : at + span] = source[...]
            stack_ref[2 * chans :, at : at + width] = edge
            stack_ref[2 * chans :, at + width : at + span] = source[:, : span - width]
        total = jnp.zeros((3 * chans, wide), F32)
        for q, source in enumerate((taps_ref, other_ref)):
            total += lax.dot_general(
                stack_ref[:, q * span : (q + 1) * span],
                source[:, width : width + span],
                NT,
                preferred_element_type=F32,
            )
        for a in range(3):
            total_ref[a] = total[a * chans : (a + 1) * chans] * scale
        for j in range(owners):

            def put(at):
                for a in range(3):
                    value = total_ref[a, at, :]
                    if j == 0:
                        keep_ref[a] = value
                    else:
                        sends[j - 1][a] = value.astype(BF)

            at_block(place(j), part, owners, 8, put)

    return call(
        body,
        [shape((3, part, wide), F32)] + [shape((3, part, wide))] * (owners - 1),
        [pltpu.VMEM((3 * chans, 2 * span), BF), pltpu.VMEM((3, chans, wide), F32)],
        12 * chans * wide * span,
        taps,
        other_taps,
        half_grad,
        other_half,
    )


def spatial_backward(pre_grad, cotangent, weights):
    rows, chans, width = pre_grad.shape

    def body(pg_ref, cot_ref, weights_ref, out_ref, taps_ref, trans_ref):
        for a in range(3):
            for b in range(3):
                at = slice(b * chans, (b + 1) * chans)
                trans_ref[a, :, at] = transposed(weights_ref[a, :, at])
        fill_taps(taps_ref, pg_ref, (1, 0, -1))

        def tile(i, carry):
            total = jnp.zeros((chans, 2 * width), F32)
            for a in range(3):
                total += jnp.dot(
                    trans_ref[a],
                    taps_ref[:, columns(2 * i + 2 - a, 2, width)],
                    preferred_element_type=F32,
                )
            for r in range(2):
                wide = cot_ref[2 * i + r].astype(F32)
                out_ref[2 * i + r] = (wide + total[:, r * width : (r + 1) * width]).astype(BF)
            return carry

        lax.fori_loop(0, rows // 2, tile, 0)

    return call(
        body,
        [shape(pre_grad.shape)],
        [
            pltpu.VMEM((3 * chans, (rows + 2) * width), BF),
            pltpu.VMEM((3, chans, 3 * chans), BF),
        ],
        18 * chans * chans * rows * width,
        pre_grad,
        cotangent,
        weights,
    )[0]


def temporal_forward(acts, cot_rows, weights, shard, scale):
    frames, rows, chans, width = cot_rows.shape
    span = rows * width
    half = shard // 2

    def body(*refs):
        act_refs = refs[:frames]
        cot_ref, weights_ref = refs[frames : frames + 2]
        outs = refs[frames + 2 : 2 * frames + 2]
        keep_ref, send_ref, flat_ref, taps_ref, cots_ref = refs[2 * frames + 2 :]
        for j, ref in enumerate(act_refs):
            for y in range(rows):
                at = pl.multiple_of(place(j) * span + y * width, width)
                flat_ref[:, pl.ds(at, width)] = ref[y]
        edge = jnp.zeros((chans, span), BF)
        whole = frames * span
        taps_ref[:chans, :span] = edge
        taps_ref[:chans, span:] = flat_ref[:, : whole - span]
        taps_ref[chans : 2 * chans, :] = flat_ref[...]
        taps_ref[2 * chans :, whole - span :] = edge
        taps_ref[2 * chans :, : whole - span] = flat_ref[:, span:]
        for f in range(frames):
            for y in range(rows):
                at = f * span + y * width
                cots_ref[:, at : at + width] = cot_ref[f, y]
        for j in range(frames):
            total = jnp.dot(
                weights_ref[...],
                taps_ref[:, columns(place(j), 1, span)],
                preferred_element_type=F32,
            ).astype(BF)
            for y in range(rows):
                outs[j][y] = total[:, y * width : (y + 1) * width]
        total = (
            lax.dot_general(cots_ref[...], taps_ref[...], NT, preferred_element_type=F32) * scale
        )
        first = core() == 0
        for s in range(chans // shard):
            low = total[s * shard : s * shard + half]
            high = total[s * shard + half : (s + 1) * shard]
            keep_ref[s] = jnp.where(first, low, high)
            send_ref[s] = jnp.where(first, high, low).astype(BF)

    owners = chans // shard
    *outs, keep, send = call(
        body,
        [shape((rows, chans, width))] * frames
        + [shape((owners, half, 3 * chans), F32), shape((owners, half, 3 * chans))],
        [
            pltpu.VMEM((chans, frames * span), BF),
            pltpu.VMEM((3 * chans, frames * span), BF),
            pltpu.VMEM((chans, frames * span), BF),
        ],
        12 * chans * cot_rows.size,
        *acts,
        cot_rows,
        weights,
    )
    return outs, keep, send


def pair_sum(keep, other):
    owners, half, wide = keep.shape

    def body(keep_ref, other_ref, own_ref, *sends):
        for j in range(owners):
            at = place(j)
            value = keep_ref[at] + other_ref[at].astype(F32)
            if j == 0:
                own_ref[...] = value
            else:
                sends[j - 1][...] = value.astype(BF)

    return call(
        body,
        [shape((half, wide), F32)] + [shape((half, wide))] * (owners - 1),
        [],
        keep.size,
        keep,
        other,
    )


def owner_sum(spatial, spatial_in, temporal, temporal_in):
    _, half, wide = spatial.shape
    count = len(spatial_in)

    def body(*refs):
        spatial_ref, temporal_ref = refs[:2]
        others, temporal_others = refs[2 : 2 + count], refs[2 + count : 2 + 2 * count]
        keep_ref, send_ref, sum_ref = refs[2 + 2 * count :]
        for a in range(3):
            value = spatial_ref[a]
            for ref in others:
                value += ref[a].astype(F32)
            sum_ref[a] = value
        value = temporal_ref[...]
        for ref in temporal_others:
            value += ref[...].astype(F32)
        sum_ref[3] = value
        bit = pair_bit()
        keep_ref[...] = sum_ref[pl.ds(2 * bit, 2)]
        send_ref[...] = sum_ref[pl.ds(2 - 2 * bit, 2)].astype(BF)

    return call(
        body,
        [shape((2, half, wide), F32), shape((2, half, wide))],
        [pltpu.VMEM((4, half, wide), F32)],
        4 * spatial.size,
        spatial,
        temporal,
        *spatial_in,
        *temporal_in,
    )


def add_rounded(keep, other):
    def body(keep_ref, other_ref, out_ref):
        out_ref[...] = (keep_ref[...].astype(F32) + other_ref[...].astype(F32)).astype(BF)

    return call(body, [shape(keep.shape)], [], keep.size, keep, other)[0]


def kernel_outputs(parts, chans):
    _, half, wide = parts[0].shape

    def body(own_ref, next_ref, core_ref, both_ref, spatial_ref, temporal_ref, sum_ref):
        bit, mine = pair_bit(), core()
        for ref, group, side in (
            (own_ref, bit, mine),
            (next_ref, 1 - bit, mine),
            (core_ref, bit, 1 - mine),
            (both_ref, 1 - bit, 1 - mine),
        ):

            def put(at):
                for g in range(2):
                    sum_ref[2 * group + g, at, :] = ref[g].astype(F32)

            at_block(side, half, 2, 8, put)
        for a in range(3):
            for b in range(3):
                spatial_ref[3 * a + b] = sum_ref[a, :, b * chans : (b + 1) * chans]
        for k in range(3):
            temporal_ref[k] = sum_ref[3, :, k * chans : (k + 1) * chans]

    return call(
        body,
        [shape((9, 2 * half, chans), F32), shape((3, 2 * half, chans), F32)],
        [pltpu.VMEM((4, 2 * half, wide), F32)],
        8 * parts[0].size,
        *parts,
    )


def block_output(frames, parts):
    rows, chans, width = frames.shape
    block = rows // len(parts)

    def body(frames_ref, *refs):
        parts_in, out_ref = refs[:-1], refs[-1]
        for j, ref in enumerate(parts_in):
            at = pl.ds(place(j) * block, block)
            out_ref[at] = (frames_ref[at].astype(F32) + ref[...].astype(F32)).astype(BF)

    return call(body, [shape(frames.shape)], [], frames.size, frames, *parts)[0]


def local(frames_in, spatial_kernel, temporal_kernel, out_cotangent):
    frames, cotangent = frames_in[0, 0], out_cotangent[0, 0]
    rows, chans, width = frames.shape
    seq, dp = lax.axis_size("seq"), lax.axis_size("dp")
    shard = spatial_kernel.shape[1]
    scale = 1.0 / math.sqrt(dp * seq * rows * width)

    first = core() == 0
    mine_a = jnp.where(first, temporal_kernel, spatial_kernel[3:6])
    mine_b = jnp.where(first, spatial_kernel[:3], spatial_kernel[6:])
    got_a = spread([mine_a] * (seq - 1))
    cot_rows = lax.all_to_all(
        cotangent.reshape(seq, rows // seq, chans, width), "seq", 0, 0, tiled=True
    )
    got_b = spread([mine_b] * (seq - 1))
    other_frames = swap(frames, "dp", 1)
    pair_a = [swap(piece, "dp", 1) for piece in got_a]
    pair_b = [swap(piece, "dp", 1) for piece in got_b]
    taps = window_taps(frames)
    other_taps = window_taps(other_frames)
    temporal_w, temporal_t = temporal_maps(temporal_kernel, got_a, pair_a)

    grads = temporal_backward(cot_rows, temporal_t)
    act_grad = [grads[0], *spread(grads[1:])]
    pre_act, weights, acts = spatial_forward(
        taps, spatial_kernel, got_a, pair_a, got_b, pair_b, rows
    )
    act_rows = [acts[0], *spread(acts[1:])]
    pre_grad, half_mine, half_theirs = activation_grad(pre_act, act_grad, shard)
    half_other = swap(half_theirs, "dp", 1)
    spatial_keep, *spatial_send = spatial_weight_grad(
        taps, other_taps, half_mine, half_other, seq, scale, width
    )
    spatial_got = spread(spatial_send)
    temporal_rows, temporal_keep, temporal_send = temporal_forward(
        act_rows, cot_rows, temporal_w, shard, scale
    )
    temporal_own, *temporal_sends = pair_sum(temporal_keep, swap(temporal_send, "dp", 1))
    temporal_got = spread(temporal_sends)
    input_grad = spatial_backward(pre_grad, cotangent, weights)
    keep, send = owner_sum(
        after(spatial_keep, input_grad), spatial_got, temporal_own, temporal_got
    )
    temporal = [temporal_rows[0], *spread(temporal_rows[1:])]
    total = add_rounded(keep, swap(send, "dp", 2))
    block_out = block_output(frames, temporal)
    bit = 4
    while bit < dp:
        total = add_rounded(total, swap(total, "dp", bit))
        bit *= 2
    total = after(total, block_out)
    near = swap(total, "dp", 2)
    spatial_grad, temporal_grad = kernel_outputs(
        (total, near, swap(total, "dp", 1), swap(near, "dp", 1)), chans
    )
    return (block_out[None, None], input_grad[None, None], spatial_grad, temporal_grad)


def solution(mesh):
    placed = (
        P("dp", "seq", None, None, None),
        P(None, "seq", None),
        P(None, "seq", None),
        P("dp", "seq", None, None, None),
    )
    return jax.shard_map(
        local,
        mesh=mesh,
        in_specs=placed,
        out_specs=(
            P("dp", "seq", None, None, None),
            P("dp", "seq", None, None, None),
            P(None, "seq", None),
            P(None, "seq", None),
        ),
        check_vma=False,
    )
```

```python
import math

import jax
import jax.numpy as jnp
from jax import lax
from jax.experimental import pallas as pl
from jax.experimental.pallas import tpu as pltpu
from jax.sharding import PartitionSpec as P

BF = jnp.bfloat16
F32 = jnp.float32
VMEM_LIMIT = 24 * 1024 * 1024
NT = (((1,), (1,)), ((), ()))


def call(body, outs, scratch, flops, *args, far=(), sent=(), light=False):
    def spec(i):
        return pl.BlockSpec(memory_space=pltpu.HBM if i in far else pltpu.VMEM)

    args = [
        pltpu.with_memory_space_constraint(arg, pltpu.HBM) if i in far else arg
        for i, arg in enumerate(args)
    ]
    factor = 0 if light else 10
    moved = sum(x.size * x.dtype.itemsize for x in (*args, *outs))
    return pl.pallas_call(
        body,
        out_shape=tuple(
            pltpu.HBM(out.shape, out.dtype) if len(args) + i in (*far, *sent) else out
            for i, out in enumerate(outs)
        ),
        in_specs=[spec(i) for i in range(len(args))],
        out_specs=tuple(spec(len(args) + i) for i in range(len(outs))),
        scratch_shapes=scratch,
        compiler_params=pltpu.CompilerParams(vmem_limit_bytes=VMEM_LIMIT),
        cost_estimate=pl.CostEstimate(flops=factor * flops + 1, bytes_accessed=factor * moved + 1, transcendentals=0),
    )(*args)


def shape(dims, dtype=BF):
    return jax.ShapeDtypeStruct(tuple(dims), dtype)


def columns(first, count, width):
    return pl.ds(pl.multiple_of(first * width, width), count * width)


def place(step):
    return jnp.bitwise_xor(lax.axis_index("seq"), step)


def core():
    return lax.rem(lax.axis_index("dp"), 2)


def pair_bit():
    return lax.rem(lax.div(lax.axis_index("dp"), 2), 2)


def at_block(index, size, count, tile, use):
    if size % tile == 0:
        use(pl.ds(pl.multiple_of(index * size, size), size))
        return
    for fixed in range(count):

        @pl.when(index == fixed)
        def _():
            use(pl.ds(fixed * size, size))


def swap(values, axis, bit):
    size = lax.axis_size(axis)
    return lax.ppermute(values, axis, [(i, i ^ bit) for i in range(size)])


def spread(blocks):
    return [swap(block, "seq", j + 1) for j, block in enumerate(blocks)]


def exchange(blocks):
    return lax.all_to_all(blocks, "seq", 0, 0, tiled=True)


def after(value, *others):
    return lax.optimization_barrier((value, *others))[0]


def shifted(block, step):
    if step == 0:
        return block
    width = block.shape[1]
    rolled = pltpu.roll(block.astype(F32), (-step) % width, 1)
    column = lax.broadcasted_iota(jnp.int32, block.shape, 1)
    edge = 0 if step < 0 else width - 1
    return jnp.where(column == edge, 0.0, rolled).astype(block.dtype)


def fill_taps(target, source, order):
    rows, chans, width = source.shape
    target[:, :width] = jnp.zeros((target.shape[0], width), target.dtype)
    target[:, (rows + 1) * width :] = jnp.zeros((target.shape[0], width), target.dtype)

    def row(y, carry):
        block = source[y]
        for b, step in enumerate(order):
            target[b * chans : (b + 1) * chans, columns(y + 1, 1, width)] = shifted(block, step)
        return carry

    lax.fori_loop(0, rows, row, 0)


def transposed(block):
    size = block.shape[0]
    one = lax.broadcasted_iota(jnp.int32, (size, size), 0) == lax.broadcasted_iota(
        jnp.int32, (size, size), 1
    )
    return lax.dot_general(one.astype(BF), block, NT, preferred_element_type=F32).astype(BF)


def window_taps(frames, light=False):
    rows, chans, width = frames.shape
    dims = (3 * chans, (rows + 2) * width)

    def body(frames_ref, far_ref, taps_ref, done):
        fill_taps(taps_ref, frames_ref, (-1, 0, 1))
        copy = pltpu.make_async_copy(taps_ref, far_ref, done)
        copy.start()
        copy.wait()

    return call(
        body,
        [shape(dims)],
        [pltpu.VMEM(dims, BF), pltpu.SemaphoreType.DMA],
        frames.size,
        frames,
        far=(1,),
        light=light,
    )[0]


def kernel_maps(own, spatial, first, second):
    _, shard, chans = own.shape
    count = len(first)

    def body(*refs):
        own_ref, spatial_ref = refs[:2]
        mine, theirs = refs[2 : 2 + count], refs[2 + count : 2 + 2 * count]
        far_trans, far_plain, far_mid, *refs = refs[2 + 2 * count :]
        trans_ref, plain_ref, mid_ref, rows_ref, done = refs

        def fill_mid(pieces):
            for j, piece in enumerate((spatial_ref, *pieces)):

                def put(at):
                    for b in range(3):
                        source = piece[3 + b] if j == 0 else piece[b]
                        mid_ref[at, b * chans : (b + 1) * chans] = source

                at_block(place(j), shard, count + 1, 16, put)

        def fill(pieces):
            for j, piece in enumerate((own_ref, *pieces)):

                def put(at):
                    for k in range(3):
                        rows_ref[k, at, :] = piece[k]

                at_block(place(j), shard, count + 1, 16, put)

        @pl.when(core() == 0)
        def _():
            fill(mine)
            fill_mid(theirs)

        @pl.when(core() == 1)
        def _():
            fill(theirs)
            fill_mid(mine)

        for k in range(3):
            plain_ref[:, k * chans : (k + 1) * chans] = rows_ref[k]
        for k in range(3):
            trans_ref[:, k * chans : (k + 1) * chans] = transposed(rows_ref[k])
        copies = [
            pltpu.make_async_copy(near, far, done.at[i])
            for i, (near, far) in enumerate(
                ((trans_ref, far_trans), (plain_ref, far_plain), (mid_ref, far_mid))
            )
        ]
        for copy in copies:
            copy.start()
        for copy in copies:
            copy.wait()

    return call(
        body,
        [shape((chans, 3 * chans))] * 3,
        [
            pltpu.VMEM((chans, 3 * chans), BF),
            pltpu.VMEM((chans, 3 * chans), BF),
            pltpu.VMEM((chans, 3 * chans), BF),
            pltpu.VMEM((3, chans, chans), BF),
            pltpu.SemaphoreType.DMA((3,)),
        ],
        6 * chans**3,
        own,
        spatial,
        *first,
        *second,
        far=(2 + 2 * count, 3 + 2 * count, 4 + 2 * count),
    )


def temporal_backward(cot_rows, weights_t):
    frames, rows, chans, width = cot_rows.shape
    span = rows * width

    def body(cot_ref, far_ref, out_ref, weights_ref, taps_ref, done):
        load = pltpu.make_async_copy(far_ref, weights_ref, done)
        load.start()
        edge = jnp.zeros((chans, span), BF)
        taps_ref[:chans, (frames - 1) * span :] = edge
        taps_ref[2 * chans :, :span] = edge
        for f in range(frames):
            for k in range(3):
                at = f + k - 1
                if 0 <= at < frames:
                    for y in range(rows):
                        to = at * span + y * width
                        taps_ref[k * chans : (k + 1) * chans, to : to + width] = cot_ref[f, y]
        load.wait()
        for f in range(frames):
            total = jnp.dot(
                weights_ref[...],
                taps_ref[:, f * span : (f + 1) * span],
                preferred_element_type=F32,
            ).astype(BF)
            for y in range(rows):
                out_ref[f, y] = total[:, y * width : (y + 1) * width]

    return call(
        body,
        [shape(cot_rows.shape)],
        [
            pltpu.VMEM(weights_t.shape, BF),
            pltpu.VMEM((3 * chans, frames * span), BF),
            pltpu.SemaphoreType.DMA,
        ],
        6 * chans * cot_rows.size,
        cot_rows,
        weights_t,
        far=(1,),
        sent=(2,),
    )[0]


def spatial_forward(taps, own, middle, pieces, rows):
    _, shard, chans = own.shape
    width = taps.shape[1] // (rows + 2)
    count = len(pieces)
    owners = count // 2 + 1
    tiles = rows // 2

    def body(*refs):
        far_taps, far_middle, far_sources = refs[0], refs[1], refs[2 : 3 + count]
        pre_ref, far_act, far_weights, taps_ref, act_ref, weights_ref, done = refs[3 + count : -2]
        own_ref, pieces_ref = refs[-2:]
        sources = [own_ref] + [pieces_ref.at[i] for i in range(count)]
        fetched = [
            pltpu.make_async_copy(far, near, done.at[tiles + 2 + i])
            for i, (far, near) in enumerate(zip(far_sources, sources))
        ]
        for copy in fetched:
            copy.start()
        middle_load = pltpu.make_async_copy(far_middle, weights_ref.at[1], done.at[tiles + 1])
        middle_load.start()

        def load(i):
            at = columns(2 * i, 2, width)
            return pltpu.make_async_copy(far_taps.at[:, at], taps_ref.at[:, at], done.at[i])

        def start(i, carry):
            load(i).start()
            return carry

        lax.fori_loop(0, tiles + 1, start, 0)

        for copy in fetched:
            copy.wait()
        lists = [sources[1 + i * (owners - 1) : 1 + (i + 1) * (owners - 1)] for i in range(2)]
        for side, order in enumerate(((0, 1), (1, 0))):

            @pl.when(core() == side)
            def _():
                for j in range(owners):

                    def put(at):
                        for a in (0, 2):
                            for b in range(3):
                                if j == 0:
                                    value = sources[0][3 * a + b]
                                else:
                                    value = lists[order[a // 2]][j - 1][b]
                                weights_ref[a, at, b * chans : (b + 1) * chans] = value

                    at_block(place(j), shard, owners, 16, put)

        middle_load.wait()
        store = pltpu.make_async_copy(weights_ref, far_weights, done.at[tiles + 1])
        store.start()
        load(jnp.int32(0)).wait()

        def act_store(i):
            at = pl.ds(2 * i, 2)
            return pltpu.make_async_copy(act_ref.at[at], far_act.at[at], done.at[i])

        def tile(i, carry):
            load(i + 1).wait()
            total = jnp.zeros((chans, 2 * width), F32)
            for a in range(3):
                total += jnp.dot(
                    weights_ref[a],
                    taps_ref[:, columns(2 * i + a, 2, width)],
                    preferred_element_type=F32,
                )
            pre = total.astype(BF)
            wide = pre.astype(F32)
            act = (wide / (1.0 + jnp.exp(-wide))).astype(BF)
            for r in range(2):
                pre_ref[2 * i + r] = pre[:, r * width : (r + 1) * width]
                act_ref[2 * i + r] = act[:, r * width : (r + 1) * width]
            act_store(i).start()
            return carry

        lax.fori_loop(0, tiles, tile, 0)

        def finish(i, carry):
            act_store(i).wait()
            return carry

        lax.fori_loop(0, tiles, finish, 0)
        store.wait()

    return call(
        body,
        [shape((rows, chans, width)), shape((rows, chans, width)), shape((3, chans, 3 * chans))],
        [
            pltpu.VMEM(taps.shape, BF),
            pltpu.VMEM((rows, chans, width), BF),
            pltpu.VMEM((3, chans, 3 * chans), BF),
            pltpu.SemaphoreType.DMA((tiles + 3 + count,)),
            pltpu.VMEM(own.shape, BF),
            pltpu.VMEM((count, 3, shard, chans), BF),
        ],
        18 * chans * chans * rows * width,
        taps,
        middle,
        own,
        *pieces,
        far=(*range(3 + count), 4 + count, 5 + count),
    )


def activation_grad(pre_act, act_grad, shard):
    rows, chans, width = pre_act.shape
    half = shard // 2

    def body(pre_ref, act_ref, mine_ref, theirs_ref, far_ref, pg_ref, done):
        def row(y, carry):
            wide = pre_ref[y].astype(F32)
            s = 1.0 / (1.0 + jnp.exp(-wide))
            pg = act_ref[y].astype(F32) * s * (1.0 + wide * (1.0 - s))
            pg_ref[y] = pg.astype(BF)
            low = [pg[at : at + half] for at in range(0, chans, shard)]
            high = [pg[at + half : at + shard] for at in range(0, chans, shard)]
            low = jnp.concatenate(low).astype(BF)
            high = jnp.concatenate(high).astype(BF)
            first = core() == 0
            mine_ref[:, columns(y, 1, width)] = jnp.where(first, low, high)
            theirs_ref[:, columns(y, 1, width)] = jnp.where(first, high, low)
            return carry

        copies = []
        for i in range(2):
            lax.fori_loop(i * rows // 2, (i + 1) * rows // 2, row, 0)
            at = pl.ds(i * rows // 2, rows // 2)
            copies.append(pltpu.make_async_copy(pg_ref.at[at], far_ref.at[at], done.at[i]))
            copies[i].start()
        for copy in copies:
            copy.wait()

    return call(
        body,
        [shape((chans // 2, rows * width))] * 2 + [shape(pre_act.shape)],
        [pltpu.VMEM(pre_act.shape, BF), pltpu.SemaphoreType.DMA((2,))],
        20 * pre_act.size,
        pre_act,
        act_grad,
        far=(4,),
    )


def spatial_weight_grad(taps, other_taps, half_grad, other_half, owners, scale, rows):
    wide = taps.shape[0]
    chans, span = half_grad.shape
    width = span // rows
    part = chans // owners

    def body(far_taps, far_other, mine_ref, theirs_ref, *refs):
        keep_ref, sends = refs[0], refs[1:owners]
        stack_ref, taps_ref, total_ref, done = refs[owners:]
        loads = [
            pltpu.make_async_copy(far, taps_ref.at[q], done.at[q])
            for q, far in enumerate((far_taps, far_other))
        ]
        for copy in loads:
            copy.start()
        edge = jnp.zeros((chans, width), BF)
        for q, source in enumerate((mine_ref, theirs_ref)):
            at = q * span
            stack_ref[:chans, at + span - width : at + span] = edge
            stack_ref[:chans, at : at + span - width] = source[:, width:]
            stack_ref[chans : 2 * chans, at : at + span] = source[...]
            stack_ref[2 * chans :, at : at + width] = edge
            stack_ref[2 * chans :, at + width : at + span] = source[:, : span - width]
        total = jnp.zeros((3 * chans, wide), F32)
        for q, copy in enumerate(loads):
            copy.wait()
            total += lax.dot_general(
                stack_ref[:, q * span : (q + 1) * span],
                taps_ref[q, :, width : width + span],
                NT,
                preferred_element_type=F32,
            )
        for a in range(3):
            total_ref[a] = total[a * chans : (a + 1) * chans] * scale
        for j in range(owners):

            def put(at):
                for a in range(3):
                    value = total_ref[a, at, :]
                    if j == 0:
                        keep_ref[a] = value
                    else:
                        sends[j - 1][a] = value.astype(BF)

            at_block(place(j), part, owners, 8, put)

    return call(
        body,
        [shape((3, part, wide), F32)] + [shape((3, part, wide))] * (owners - 1),
        [
            pltpu.VMEM((3 * chans, 2 * span), BF),
            pltpu.VMEM((2,) + taps.shape, BF),
            pltpu.VMEM((3, chans, wide), F32),
            pltpu.SemaphoreType.DMA((2,)),
        ],
        12 * chans * wide * span,
        taps,
        other_taps,
        half_grad,
        other_half,
        far=(0, 1),
        sent=tuple(range(5, 4 + owners)),
        light=True,
    )


def spatial_backward(pre_grad, cotangent, weights):
    rows, chans, width = pre_grad.shape

    def body(far_pg, far_cot, far_weights, out_ref, *refs):
        pg_ref, cot_ref, weights_ref, taps_ref, trans_ref, done = refs
        loads = [
            pltpu.make_async_copy(far, near, done.at[i])
            for i, (far, near) in enumerate(
                ((far_pg, pg_ref), (far_weights, weights_ref), (far_cot, cot_ref))
            )
        ]
        for copy in loads:
            copy.start()
        loads[0].wait()
        fill_taps(taps_ref, pg_ref, (1, 0, -1))
        loads[1].wait()
        for a in range(3):
            for b in range(3):
                at = slice(b * chans, (b + 1) * chans)
                trans_ref[a, :, at] = transposed(weights_ref[a, :, at])
        loads[2].wait()

        def tile(i, carry):
            total = jnp.zeros((chans, 2 * width), F32)
            for a in range(3):
                total += jnp.dot(
                    trans_ref[a],
                    taps_ref[:, columns(2 * i + 2 - a, 2, width)],
                    preferred_element_type=F32,
                )
            for r in range(2):
                wide = cot_ref[2 * i + r].astype(F32)
                out_ref[2 * i + r] = (wide + total[:, r * width : (r + 1) * width]).astype(BF)
            return carry

        lax.fori_loop(0, rows // 2, tile, 0)

    return call(
        body,
        [shape(pre_grad.shape)],
        [
            pltpu.VMEM(pre_grad.shape, BF),
            pltpu.VMEM(pre_grad.shape, BF),
            pltpu.VMEM((3, chans, 3 * chans), BF),
            pltpu.VMEM((3 * chans, (rows + 2) * width), BF),
            pltpu.VMEM((3, chans, 3 * chans), BF),
            pltpu.SemaphoreType.DMA((3,)),
        ],
        18 * chans * chans * rows * width,
        pre_grad,
        cotangent,
        weights,
        far=(0, 1, 2),
    )[0]


def temporal_forward(acts, cot_rows, weights, shard, scale):
    frames, rows, chans, width = cot_rows.shape
    span = rows * width
    half = shard // 2

    def body(act_ref, cot_ref, far_ref, out_ref, keep_ref, send_ref, *refs):
        weights_ref, taps_ref, cots_ref, done = refs
        load = pltpu.make_async_copy(far_ref, weights_ref, done)
        load.start()
        edge = jnp.zeros((chans, span), BF)
        taps_ref[:chans, :span] = edge
        taps_ref[2 * chans :, (frames - 1) * span :] = edge
        for f in range(frames):
            for y in range(rows):
                at = f * span + y * width
                cots_ref[:, at : at + width] = cot_ref[f, y]
                for k in range(3):
                    if 0 <= f - k + 1 < frames:
                        to = at + (1 - k) * span
                        taps_ref[k * chans : (k + 1) * chans, to : to + width] = act_ref[f, y]
        load.wait()
        for f in range(frames):
            total = jnp.dot(
                weights_ref[...],
                taps_ref[:, f * span : (f + 1) * span],
                preferred_element_type=F32,
            ).astype(BF)
            for y in range(rows):
                out_ref[f, y] = total[:, y * width : (y + 1) * width]
        total = (
            lax.dot_general(cots_ref[...], taps_ref[...], NT, preferred_element_type=F32) * scale
        )
        first = core() == 0
        for s in range(chans // shard):
            low = total[s * shard : s * shard + half]
            high = total[s * shard + half : (s + 1) * shard]
            keep_ref[s] = jnp.where(first, low, high)
            send_ref[s] = jnp.where(first, high, low).astype(BF)

    owners = chans // shard
    return call(
        body,
        [
            shape(cot_rows.shape),
            shape((owners, half, 3 * chans), F32),
            shape((owners, half, 3 * chans)),
        ],
        [
            pltpu.VMEM(weights.shape, BF),
            pltpu.VMEM((3 * chans, frames * span), BF),
            pltpu.VMEM((chans, frames * span), BF),
            pltpu.SemaphoreType.DMA,
        ],
        12 * chans * cot_rows.size,
        acts,
        cot_rows,
        weights,
        far=(2,),
        sent=(3,),
    )


def owner_sum(spatial, others, temporal):
    _, half, wide = spatial.shape
    count = len(others)

    def body(spatial_ref, temporal_ref, *refs):
        other_refs, (keep_ref, send_ref, sum_ref) = refs[:count], refs[count:]
        for a in range(3):
            value = spatial_ref[a]
            for ref in other_refs:
                value += ref[a].astype(F32)
            sum_ref[a] = value
        value = temporal_ref[0].astype(F32)
        for s in range(1, count + 1):
            value += temporal_ref[s].astype(F32)
        sum_ref[3] = value
        bit = pair_bit()
        keep_ref[...] = sum_ref[pl.ds(2 * bit, 2)]
        send_ref[...] = sum_ref[pl.ds(2 - 2 * bit, 2)].astype(BF)

    return call(
        body,
        [shape((2, half, wide), F32), shape((2, half, wide))],
        [pltpu.VMEM((4, half, wide), F32)],
        4 * spatial.size,
        spatial,
        temporal,
        *others,
    )


def add_rounded(keep, other):
    def body(keep_ref, other_ref, out_ref):
        out_ref[...] = (keep_ref[...].astype(F32) + other_ref[...].astype(F32)).astype(BF)

    return call(body, [shape(keep.shape)], [], keep.size, keep, other)[0]


def kernel_outputs(parts, chans):
    _, half, wide = parts[0].shape

    def body(own_ref, next_ref, core_ref, both_ref, spatial_ref, temporal_ref, sum_ref):
        bit, mine = pair_bit(), core()
        for ref, group, side in (
            (own_ref, bit, mine),
            (next_ref, 1 - bit, mine),
            (core_ref, bit, 1 - mine),
            (both_ref, 1 - bit, 1 - mine),
        ):

            def put(at):
                for g in range(2):
                    sum_ref[2 * group + g, at, :] = ref[g].astype(F32)

            at_block(side, half, 2, 8, put)
        for a in range(3):
            for b in range(3):
                spatial_ref[3 * a + b] = sum_ref[a, :, b * chans : (b + 1) * chans]
        for k in range(3):
            temporal_ref[k] = sum_ref[3, :, k * chans : (k + 1) * chans]

    return call(
        body,
        [shape((9, 2 * half, chans), F32), shape((3, 2 * half, chans), F32)],
        [pltpu.VMEM((4, 2 * half, wide), F32)],
        8 * parts[0].size,
        *parts,
    )


def block_output(frames, temporal):
    def body(frames_ref, temporal_ref, out_ref):
        out_ref[...] = (frames_ref[...].astype(F32) + temporal_ref[...].astype(F32)).astype(BF)

    return call(body, [shape(frames.shape)], [], frames.size, frames, temporal)[0]


def local(frames_in, spatial_kernel, temporal_kernel, out_cotangent):
    frames, cotangent = frames_in[0, 0], out_cotangent[0, 0]
    rows, chans, width = frames.shape
    seq, dp = lax.axis_size("seq"), lax.axis_size("dp")
    shard = spatial_kernel.shape[1]
    scale = 1.0 / math.sqrt(dp * seq * rows * width)

    first = core() == 0
    mine_a = jnp.where(first, temporal_kernel, spatial_kernel[3:6])
    mine_b = jnp.where(first, spatial_kernel[:3], spatial_kernel[6:])
    got_a = spread([mine_a] * (seq - 1))
    cot_rows = exchange(cotangent.reshape(seq, rows // seq, chans, width))
    got_b = spread([mine_b] * (seq - 1))
    pair_a = [swap(piece, "dp", 1) for piece in got_a]
    temporal_t, temporal_w, middle = kernel_maps(
        temporal_kernel, spatial_kernel, got_a, pair_a
    )
    taps = window_taps(frames)
    temporal_t, taps = lax.optimization_barrier((temporal_t, taps))
    grad_rows = temporal_backward(cot_rows, temporal_t)
    act_grad = exchange(grad_rows).reshape(frames.shape)
    grad_rows, *got_b = lax.optimization_barrier((grad_rows, *got_b))
    pair_b = [swap(piece, "dp", 1) for piece in got_b]
    other_frames = swap(after(frames, middle), "dp", 1)
    pre_act, activated, weights = spatial_forward(
        taps, spatial_kernel, middle, (*got_b, *pair_b), rows
    )
    half_mine, half_theirs, pre_grad = activation_grad(pre_act, act_grad, shard)
    half_other = swap(half_theirs, "dp", 1)
    other_taps = window_taps(after(other_frames, half_theirs), light=True)
    act_rows = exchange(activated.reshape(cot_rows.shape))
    spatial_keep, *spatial_send = spatial_weight_grad(
        taps, other_taps, half_mine, half_other, seq, scale, rows
    )
    spatial_got = spread(spatial_send)
    temporal_rows, temporal_keep, temporal_send = temporal_forward(
        act_rows, cot_rows, after(temporal_w, spatial_keep), shard, scale
    )
    temporal_part = exchange(add_rounded(temporal_keep, swap(temporal_send, "dp", 1)))
    keep, send = owner_sum(spatial_keep, spatial_got, temporal_part)
    temporal_rows = exchange(after(temporal_rows, keep)).reshape(frames.shape)
    total = add_rounded(keep, swap(send, "dp", 2))
    input_grad = spatial_backward(after(pre_grad, keep), cotangent, weights)
    bit = 4
    while bit < dp:
        other = swap(total, "dp", bit)
        total = add_rounded(after(total, input_grad), other)
        bit *= 2
    block_out = block_output(frames, temporal_rows)
    near = swap(total, "dp", 2)
    near, block_out = lax.optimization_barrier((near, block_out))
    spatial_grad, temporal_grad = kernel_outputs(
        (total, near, swap(total, "dp", 1), swap(near, "dp", 1)), chans
    )
    return (block_out[None, None], input_grad[None, None], spatial_grad, temporal_grad)


def solution(mesh):
    placed = (
        P("dp", "seq", None, None, None),
        P(None, "seq", None),
        P(None, "seq", None),
        P("dp", "seq", None, None, None),
    )
    return jax.shard_map(
        local,
        mesh=mesh,
        in_specs=placed,
        out_specs=(
            P("dp", "seq", None, None, None),
            P("dp", "seq", None, None, None),
            P(None, "seq", None),
            P(None, "seq", None),
        ),
        check_vma=False,
    )
```

```python
import math

import jax
import jax.numpy as jnp
from jax import lax
from jax.experimental import pallas as pl
from jax.experimental.pallas import tpu as pltpu
from jax.sharding import PartitionSpec as P

BF = jnp.bfloat16
F32 = jnp.float32
VMEM_LIMIT = 24 * 1024 * 1024
NT = (((1,), (1,)), ((), ()))


def call(body, outs, scratch, flops, *args, far=(), sent=(), weight=10):
    def spec(i):
        return pl.BlockSpec(memory_space=pltpu.HBM if i in far else pltpu.VMEM)

    args = [
        pltpu.with_memory_space_constraint(arg, pltpu.HBM) if i in far else arg
        for i, arg in enumerate(args)
    ]
    moved = sum(x.size * x.dtype.itemsize for x in (*args, *outs))
    return pl.pallas_call(
        body,
        out_shape=tuple(
            pltpu.HBM(out.shape, out.dtype) if len(args) + i in (*far, *sent) else out
            for i, out in enumerate(outs)
        ),
        in_specs=[spec(i) for i in range(len(args))],
        out_specs=tuple(spec(len(args) + i) for i in range(len(outs))),
        scratch_shapes=scratch,
        compiler_params=pltpu.CompilerParams(vmem_limit_bytes=VMEM_LIMIT),
        cost_estimate=pl.CostEstimate(flops=weight * flops + 1, bytes_accessed=weight * moved + 1, transcendentals=0),
    )(*args)


def shape(dims, dtype=BF):
    return jax.ShapeDtypeStruct(tuple(dims), dtype)


def columns(first, count, width):
    return pl.ds(pl.multiple_of(first * width, width), count * width)


def place(step):
    return jnp.bitwise_xor(lax.axis_index("seq"), step)


def core():
    return lax.rem(lax.axis_index("dp"), 2)


def pair_bit():
    return lax.rem(lax.div(lax.axis_index("dp"), 2), 2)


def at_block(index, size, count, tile, use):
    if size % tile == 0:
        use(pl.ds(pl.multiple_of(index * size, size), size))
        return
    for fixed in range(count):

        @pl.when(index == fixed)
        def _():
            use(pl.ds(fixed * size, size))


def swap(values, axis, bit):
    size = lax.axis_size(axis)
    return lax.ppermute(values, axis, [(i, i ^ bit) for i in range(size)])


def spread(blocks):
    return [swap(block, "seq", j + 1) for j, block in enumerate(blocks)]


def exchange(blocks):
    return lax.all_to_all(blocks, "seq", 0, 0, tiled=True)


def after(value, *others):
    return lax.optimization_barrier((value, *others))[0]


def shifted(block, step):
    if step == 0:
        return block
    width = block.shape[1]
    rolled = pltpu.roll(block.astype(F32), (-step) % width, 1)
    column = lax.broadcasted_iota(jnp.int32, block.shape, 1)
    edge = 0 if step < 0 else width - 1
    return jnp.where(column == edge, 0.0, rolled).astype(block.dtype)


def fill_taps(target, source, order):
    rows, chans, width = source.shape
    target[:, :width] = jnp.zeros((target.shape[0], width), target.dtype)
    target[:, (rows + 1) * width :] = jnp.zeros((target.shape[0], width), target.dtype)

    def row(y, carry):
        block = source[y]
        for b, step in enumerate(order):
            target[b * chans : (b + 1) * chans, columns(y + 1, 1, width)] = shifted(block, step)
        return carry

    lax.fori_loop(0, rows, row, 0)


def transposed(block):
    size = block.shape[0]
    one = lax.broadcasted_iota(jnp.int32, (size, size), 0) == lax.broadcasted_iota(
        jnp.int32, (size, size), 1
    )
    return lax.dot_general(one.astype(BF), block, NT, preferred_element_type=F32).astype(BF)


def window_taps(frames, weight=10):
    rows, chans, width = frames.shape
    dims = (3 * chans, (rows + 2) * width)

    def body(frames_ref, far_ref, taps_ref, done):
        fill_taps(taps_ref, frames_ref, (-1, 0, 1))
        copy = pltpu.make_async_copy(taps_ref, far_ref, done)
        copy.start()
        copy.wait()

    return call(
        body,
        [shape(dims)],
        [pltpu.VMEM(dims, BF), pltpu.SemaphoreType.DMA],
        frames.size,
        frames,
        far=(1,),
        weight=weight,
    )[0]


def kernel_maps(own, spatial, first, second):
    _, shard, chans = own.shape
    count = len(first)

    def body(*refs):
        own_ref, spatial_ref = refs[:2]
        mine, theirs = refs[2 : 2 + count], refs[2 + count : 2 + 2 * count]
        far_trans, far_plain, far_mid, *refs = refs[2 + 2 * count :]
        trans_ref, plain_ref, mid_ref, rows_ref, done = refs

        def fill_mid(pieces):
            for j, piece in enumerate((spatial_ref, *pieces)):

                def put(at):
                    for b in range(3):
                        source = piece[3 + b] if j == 0 else piece[b]
                        mid_ref[at, b * chans : (b + 1) * chans] = source

                at_block(place(j), shard, count + 1, 16, put)

        def fill(pieces):
            for j, piece in enumerate((own_ref, *pieces)):

                def put(at):
                    for k in range(3):
                        rows_ref[k, at, :] = piece[k]

                at_block(place(j), shard, count + 1, 16, put)

        @pl.when(core() == 0)
        def _():
            fill(mine)
            fill_mid(theirs)

        @pl.when(core() == 1)
        def _():
            fill(theirs)
            fill_mid(mine)

        for k in range(3):
            plain_ref[:, k * chans : (k + 1) * chans] = rows_ref[k]
        for k in range(3):
            trans_ref[:, k * chans : (k + 1) * chans] = transposed(rows_ref[k])
        copies = [
            pltpu.make_async_copy(near, far, done.at[i])
            for i, (near, far) in enumerate(
                ((trans_ref, far_trans), (plain_ref, far_plain), (mid_ref, far_mid))
            )
        ]
        for copy in copies:
            copy.start()
        for copy in copies:
            copy.wait()

    return call(
        body,
        [shape((chans, 3 * chans))] * 3,
        [
            pltpu.VMEM((chans, 3 * chans), BF),
            pltpu.VMEM((chans, 3 * chans), BF),
            pltpu.VMEM((chans, 3 * chans), BF),
            pltpu.VMEM((3, chans, chans), BF),
            pltpu.SemaphoreType.DMA((3,)),
        ],
        6 * chans**3,
        own,
        spatial,
        *first,
        *second,
        far=(2 + 2 * count, 3 + 2 * count, 4 + 2 * count),
    )


def temporal_backward(cot_rows, weights_t):
    frames, rows, chans, width = cot_rows.shape
    span = rows * width

    def body(cot_ref, far_ref, *refs):
        outs, (weights_ref, taps_ref, done) = refs[:frames], refs[frames:]
        load = pltpu.make_async_copy(far_ref, weights_ref, done)
        load.start()
        edge = jnp.zeros((chans, span), BF)
        taps_ref[:chans, (frames - 1) * span :] = edge
        taps_ref[2 * chans :, :span] = edge
        for f in range(frames):
            for k in range(3):
                at = f + k - 1
                if 0 <= at < frames:
                    for y in range(rows):
                        to = at * span + y * width
                        taps_ref[k * chans : (k + 1) * chans, to : to + width] = cot_ref[f, y]
        load.wait()
        for j in range(frames):
            total = jnp.dot(
                weights_ref[...],
                taps_ref[:, columns(place(j), 1, span)],
                preferred_element_type=F32,
            ).astype(BF)
            for y in range(rows):
                outs[j][y] = total[:, y * width : (y + 1) * width]

    return call(
        body,
        [shape((rows, chans, width))] * frames,
        [
            pltpu.VMEM(weights_t.shape, BF),
            pltpu.VMEM((3 * chans, frames * span), BF),
            pltpu.SemaphoreType.DMA,
        ],
        6 * chans * cot_rows.size,
        cot_rows,
        weights_t,
        far=(1,),
        sent=tuple(range(2, 2 + frames)),
    )


def spatial_forward(taps, own, middle, pieces, rows):
    _, shard, chans = own.shape
    width = taps.shape[1] // (rows + 2)
    count = len(pieces)
    owners = count // 2 + 1
    tiles = rows // 2

    def body(*refs):
        far_taps, far_middle, far_sources = refs[0], refs[1], refs[2 : 3 + count]
        pre_ref, far_act, far_weights, taps_ref, act_ref, weights_ref, done = refs[3 + count : -2]
        own_ref, pieces_ref = refs[-2:]
        sources = [own_ref] + [pieces_ref.at[i] for i in range(count)]
        fetched = [
            pltpu.make_async_copy(far, near, done.at[tiles + 2 + i])
            for i, (far, near) in enumerate(zip(far_sources, sources))
        ]
        for copy in fetched:
            copy.start()
        middle_load = pltpu.make_async_copy(far_middle, weights_ref.at[1], done.at[tiles + 1])
        middle_load.start()

        def load(i):
            at = columns(2 * i, 2, width)
            return pltpu.make_async_copy(far_taps.at[:, at], taps_ref.at[:, at], done.at[i])

        def start(i, carry):
            load(i).start()
            return carry

        lax.fori_loop(0, tiles + 1, start, 0)

        for copy in fetched:
            copy.wait()
        lists = [sources[1 + i * (owners - 1) : 1 + (i + 1) * (owners - 1)] for i in range(2)]
        for side, order in enumerate(((0, 1), (1, 0))):

            @pl.when(core() == side)
            def _():
                for j in range(owners):

                    def put(at):
                        for a in (0, 2):
                            for b in range(3):
                                if j == 0:
                                    value = sources[0][3 * a + b]
                                else:
                                    value = lists[order[a // 2]][j - 1][b]
                                weights_ref[a, at, b * chans : (b + 1) * chans] = value

                    at_block(place(j), shard, owners, 16, put)

        middle_load.wait()
        store = pltpu.make_async_copy(weights_ref, far_weights, done.at[tiles + 1])
        store.start()
        load(jnp.int32(0)).wait()

        def act_store(i):
            at = pl.ds(2 * i, 2)
            return pltpu.make_async_copy(act_ref.at[at], far_act.at[at], done.at[i])

        def tile(i, carry):
            load(i + 1).wait()
            total = jnp.zeros((chans, 2 * width), F32)
            for a in range(3):
                total += jnp.dot(
                    weights_ref[a],
                    taps_ref[:, columns(2 * i + a, 2, width)],
                    preferred_element_type=F32,
                )
            pre = total.astype(BF)
            wide = pre.astype(F32)
            act = (wide / (1.0 + jnp.exp(-wide))).astype(BF)
            for r in range(2):
                pre_ref[2 * i + r] = pre[:, r * width : (r + 1) * width]
                act_ref[2 * i + r] = act[:, r * width : (r + 1) * width]
            act_store(i).start()
            return carry

        lax.fori_loop(0, tiles, tile, 0)

        def finish(i, carry):
            act_store(i).wait()
            return carry

        lax.fori_loop(0, tiles, finish, 0)
        store.wait()

    return call(
        body,
        [shape((rows, chans, width)), shape((rows, chans, width)), shape((3, chans, 3 * chans))],
        [
            pltpu.VMEM(taps.shape, BF),
            pltpu.VMEM((rows, chans, width), BF),
            pltpu.VMEM((3, chans, 3 * chans), BF),
            pltpu.SemaphoreType.DMA((tiles + 3 + count,)),
            pltpu.VMEM(own.shape, BF),
            pltpu.VMEM((count, 3, shard, chans), BF),
        ],
        18 * chans * chans * rows * width,
        taps,
        middle,
        own,
        *pieces,
        far=(*range(3 + count), 4 + count, 5 + count),
        weight=10,
    )


def activation_grad(pre_act, grads, shard):
    rows, chans, width = pre_act.shape
    half = shard // 2

    block = rows // len(grads)

    def body(pre_ref, *refs):
        grad_refs, refs = refs[: len(grads)], refs[len(grads) :]
        mine_ref, theirs_ref, far_ref, pg_ref, act_ref, done = refs
        for j, ref in enumerate(grad_refs):
            act_ref[pl.ds(place(j) * block, block)] = ref[...]

        def row(y, carry):
            wide = pre_ref[y].astype(F32)
            s = 1.0 / (1.0 + jnp.exp(-wide))
            pg = act_ref[y].astype(F32) * s * (1.0 + wide * (1.0 - s))
            pg_ref[y] = pg.astype(BF)
            low = [pg[at : at + half] for at in range(0, chans, shard)]
            high = [pg[at + half : at + shard] for at in range(0, chans, shard)]
            low = jnp.concatenate(low).astype(BF)
            high = jnp.concatenate(high).astype(BF)
            first = core() == 0
            mine_ref[:, columns(y, 1, width)] = jnp.where(first, low, high)
            theirs_ref[:, columns(y, 1, width)] = jnp.where(first, high, low)
            return carry

        copies = []
        for i in range(2):
            lax.fori_loop(i * rows // 2, (i + 1) * rows // 2, row, 0)
            at = pl.ds(i * rows // 2, rows // 2)
            copies.append(pltpu.make_async_copy(pg_ref.at[at], far_ref.at[at], done.at[i]))
            copies[i].start()
        for copy in copies:
            copy.wait()

    return call(
        body,
        [shape((chans // 2, rows * width))] * 2 + [shape(pre_act.shape)],
        [
            pltpu.VMEM(pre_act.shape, BF),
            pltpu.VMEM(pre_act.shape, BF),
            pltpu.SemaphoreType.DMA((2,)),
        ],
        20 * pre_act.size,
        pre_act,
        *grads,
        far=(3 + len(grads),),
    )


def spatial_weight_grad(taps, other_taps, half_grad, other_half, owners, scale, rows):
    wide = taps.shape[0]
    chans, span = half_grad.shape
    width = span // rows
    part = chans // owners

    def body(far_taps, far_other, mine_ref, theirs_ref, *refs):
        keep_ref, sends = refs[0], refs[1:owners]
        stack_ref, taps_ref, total_ref, done = refs[owners:]
        loads = [
            pltpu.make_async_copy(far, taps_ref.at[q], done.at[q])
            for q, far in enumerate((far_taps, far_other))
        ]
        for copy in loads:
            copy.start()
        edge = jnp.zeros((chans, width), BF)
        for q, source in enumerate((mine_ref, theirs_ref)):
            at = q * span
            stack_ref[:chans, at + span - width : at + span] = edge
            stack_ref[:chans, at : at + span - width] = source[:, width:]
            stack_ref[chans : 2 * chans, at : at + span] = source[...]
            stack_ref[2 * chans :, at : at + width] = edge
            stack_ref[2 * chans :, at + width : at + span] = source[:, : span - width]
        total = jnp.zeros((3 * chans, wide), F32)
        for q, copy in enumerate(loads):
            copy.wait()
            total += lax.dot_general(
                stack_ref[:, q * span : (q + 1) * span],
                taps_ref[q, :, width : width + span],
                NT,
                preferred_element_type=F32,
            )
        for a in range(3):
            total_ref[a] = total[a * chans : (a + 1) * chans] * scale
        for j in range(owners):

            def put(at):
                for a in range(3):
                    value = total_ref[a, at, :]
                    if j == 0:
                        keep_ref[a] = value
                    else:
                        sends[j - 1][a] = value.astype(BF)

            at_block(place(j), part, owners, 8, put)

    return call(
        body,
        [shape((3, part, wide), F32)] + [shape((3, part, wide))] * (owners - 1),
        [
            pltpu.VMEM((3 * chans, 2 * span), BF),
            pltpu.VMEM((2,) + taps.shape, BF),
            pltpu.VMEM((3, chans, wide), F32),
            pltpu.SemaphoreType.DMA((2,)),
        ],
        12 * chans * wide * span,
        taps,
        other_taps,
        half_grad,
        other_half,
        far=(0, 1),
        sent=tuple(range(5, 4 + owners)),
        weight=0,
    )


def spatial_backward(pre_grad, cotangent, weights):
    rows, chans, width = pre_grad.shape

    def body(far_pg, far_cot, far_weights, out_ref, *refs):
        pg_ref, cot_ref, weights_ref, taps_ref, trans_ref, done = refs
        loads = [
            pltpu.make_async_copy(far, near, done.at[i])
            for i, (far, near) in enumerate(
                ((far_pg, pg_ref), (far_weights, weights_ref), (far_cot, cot_ref))
            )
        ]
        for copy in loads:
            copy.start()
        loads[0].wait()
        fill_taps(taps_ref, pg_ref, (1, 0, -1))
        loads[1].wait()
        for a in range(3):
            for b in range(3):
                at = slice(b * chans, (b + 1) * chans)
                trans_ref[a, :, at] = transposed(weights_ref[a, :, at])
        loads[2].wait()

        def tile(i, carry):
            total = jnp.zeros((chans, 2 * width), F32)
            for a in range(3):
                total += jnp.dot(
                    trans_ref[a],
                    taps_ref[:, columns(2 * i + 2 - a, 2, width)],
                    preferred_element_type=F32,
                )
            for r in range(2):
                wide = cot_ref[2 * i + r].astype(F32)
                out_ref[2 * i + r] = (wide + total[:, r * width : (r + 1) * width]).astype(BF)
            return carry

        lax.fori_loop(0, rows // 2, tile, 0)

    return call(
        body,
        [shape(pre_grad.shape)],
        [
            pltpu.VMEM(pre_grad.shape, BF),
            pltpu.VMEM(pre_grad.shape, BF),
            pltpu.VMEM((3, chans, 3 * chans), BF),
            pltpu.VMEM((3 * chans, (rows + 2) * width), BF),
            pltpu.VMEM((3, chans, 3 * chans), BF),
            pltpu.SemaphoreType.DMA((3,)),
        ],
        18 * chans * chans * rows * width,
        pre_grad,
        cotangent,
        weights,
        far=(0, 1, 2),
    )[0]


def temporal_weight_grad(acts, cot_rows, shard, scale):
    frames, rows, chans, width = cot_rows.shape
    span = rows * width
    half = shard // 2
    owners = chans // shard

    def body(act_ref, cot_ref, keep_ref, send_ref, taps_ref, cots_ref):
        edge = jnp.zeros((chans, span), BF)
        taps_ref[:chans, :span] = edge
        taps_ref[2 * chans :, (frames - 1) * span :] = edge
        for f in range(frames):
            for y in range(rows):
                at = f * span + y * width
                cots_ref[:, at : at + width] = cot_ref[f, y]
                for k in range(3):
                    if 0 <= f - k + 1 < frames:
                        to = at + (1 - k) * span
                        taps_ref[k * chans : (k + 1) * chans, to : to + width] = act_ref[f, y]
        total = (
            lax.dot_general(cots_ref[...], taps_ref[...], NT, preferred_element_type=F32) * scale
        )
        first = core() == 0
        for s in range(owners):
            low = total[s * shard : s * shard + half]
            high = total[s * shard + half : (s + 1) * shard]
            keep_ref[s] = jnp.where(first, low, high)
            send_ref[s] = jnp.where(first, high, low).astype(BF)

    return call(
        body,
        [shape((owners, half, 3 * chans), F32), shape((owners, half, 3 * chans))],
        [
            pltpu.VMEM((3 * chans, frames * span), BF),
            pltpu.VMEM((chans, frames * span), BF),
        ],
        6 * chans * cot_rows.size,
        acts,
        cot_rows,
    )


def temporal_forward(acts, weights):
    frames, rows, chans, width = acts.shape
    span = rows * width

    def body(act_ref, far_ref, out_ref, weights_ref, taps_ref, done):
        load = pltpu.make_async_copy(far_ref, weights_ref, done)
        load.start()
        edge = jnp.zeros((chans, span), BF)
        taps_ref[:chans, :span] = edge
        taps_ref[2 * chans :, (frames - 1) * span :] = edge
        for f in range(frames):
            for k in range(3):
                if 0 <= f - k + 1 < frames:
                    for y in range(rows):
                        to = (f - k + 1) * span + y * width
                        taps_ref[k * chans : (k + 1) * chans, to : to + width] = act_ref[f, y]
        load.wait()
        for f in range(frames):
            total = jnp.dot(
                weights_ref[...],
                taps_ref[:, f * span : (f + 1) * span],
                preferred_element_type=F32,
            ).astype(BF)
            for y in range(rows):
                out_ref[f, y] = total[:, y * width : (y + 1) * width]

    return call(
        body,
        [shape(acts.shape)],
        [
            pltpu.VMEM(weights.shape, BF),
            pltpu.VMEM((3 * chans, frames * span), BF),
            pltpu.SemaphoreType.DMA,
        ],
        6 * chans * acts.size,
        acts,
        weights,
        far=(1,),
        sent=(2,),
    )[0]


def owner_sum(spatial, others, temporal):
    _, half, wide = spatial.shape
    count = len(others)

    def body(spatial_ref, temporal_ref, *refs):
        other_refs, (keep_ref, send_ref, sum_ref) = refs[:count], refs[count:]
        for a in range(3):
            value = spatial_ref[a]
            for ref in other_refs:
                value += ref[a].astype(F32)
            sum_ref[a] = value
        value = temporal_ref[0].astype(F32)
        for s in range(1, count + 1):
            value += temporal_ref[s].astype(F32)
        sum_ref[3] = value
        bit = pair_bit()
        keep_ref[...] = sum_ref[pl.ds(2 * bit, 2)]
        send_ref[...] = sum_ref[pl.ds(2 - 2 * bit, 2)].astype(BF)

    return call(
        body,
        [shape((2, half, wide), F32), shape((2, half, wide))],
        [pltpu.VMEM((4, half, wide), F32)],
        4 * spatial.size,
        spatial,
        temporal,
        *others,
    )


def add_rounded(keep, other):
    def body(keep_ref, other_ref, out_ref):
        out_ref[...] = (keep_ref[...].astype(F32) + other_ref[...].astype(F32)).astype(BF)

    return call(body, [shape(keep.shape)], [], keep.size, keep, other)[0]


def kernel_outputs(parts, chans):
    _, half, wide = parts[0].shape

    def body(own_ref, next_ref, core_ref, both_ref, spatial_ref, temporal_ref, sum_ref):
        bit, mine = pair_bit(), core()
        for ref, group, side in (
            (own_ref, bit, mine),
            (next_ref, 1 - bit, mine),
            (core_ref, bit, 1 - mine),
            (both_ref, 1 - bit, 1 - mine),
        ):

            def put(at):
                for g in range(2):
                    sum_ref[2 * group + g, at, :] = ref[g].astype(F32)

            at_block(side, half, 2, 8, put)
        for a in range(3):
            for b in range(3):
                spatial_ref[3 * a + b] = sum_ref[a, :, b * chans : (b + 1) * chans]
        for k in range(3):
            temporal_ref[k] = sum_ref[3, :, k * chans : (k + 1) * chans]

    return call(
        body,
        [shape((9, 2 * half, chans), F32), shape((3, 2 * half, chans), F32)],
        [pltpu.VMEM((4, 2 * half, wide), F32)],
        8 * parts[0].size,
        *parts,
    )


def block_output(frames, temporal):
    def body(frames_ref, temporal_ref, out_ref):
        out_ref[...] = (frames_ref[...].astype(F32) + temporal_ref[...].astype(F32)).astype(BF)

    return call(body, [shape(frames.shape)], [], frames.size, frames, temporal)[0]


def local(frames_in, spatial_kernel, temporal_kernel, out_cotangent):
    frames, cotangent = frames_in[0, 0], out_cotangent[0, 0]
    rows, chans, width = frames.shape
    seq, dp = lax.axis_size("seq"), lax.axis_size("dp")
    shard = spatial_kernel.shape[1]
    scale = 1.0 / math.sqrt(dp * seq * rows * width)

    first = core() == 0
    mine_a = jnp.where(first, temporal_kernel, spatial_kernel[3:6])
    mine_b = jnp.where(first, spatial_kernel[:3], spatial_kernel[6:])
    got_a = spread([mine_a] * (seq - 1))
    cot_rows = exchange(cotangent.reshape(seq, rows // seq, chans, width))
    got_b = spread([mine_b] * (seq - 1))
    pair_a = [swap(piece, "dp", 1) for piece in got_a]
    temporal_t, temporal_w, middle = kernel_maps(
        temporal_kernel, spatial_kernel, got_a, pair_a
    )
    taps = window_taps(frames)
    temporal_t, taps = lax.optimization_barrier((temporal_t, taps))
    grad_rows = temporal_backward(cot_rows, temporal_t)
    act_grad = [grad_rows[0], *spread(grad_rows[1:])]
    temporal_w, *got_b = lax.optimization_barrier((after(temporal_w, grad_rows[0]), *got_b))
    pair_b = [swap(piece, "dp", 1) for piece in got_b]
    other_frames = swap(after(frames, middle), "dp", 1)
    pre_act, activated, weights = spatial_forward(
        taps, spatial_kernel, middle, (*got_b, *pair_b), rows
    )
    half_mine, half_theirs, pre_grad = activation_grad(pre_act, act_grad, shard)
    half_other = swap(half_theirs, "dp", 1)
    other_taps = window_taps(after(other_frames, half_theirs), weight=0)
    act_rows = exchange(activated.reshape(cot_rows.shape))
    spatial_keep, *spatial_send = spatial_weight_grad(
        taps, other_taps, half_mine, half_other, seq, scale, rows
    )
    spatial_got = spread(spatial_send)
    temporal_keep, temporal_send = temporal_weight_grad(
        act_rows, after(cot_rows, spatial_keep), shard, scale
    )
    temporal_part = add_rounded(temporal_keep, swap(temporal_send, "dp", 1))
    temporal_rows = temporal_forward(act_rows, after(temporal_w, temporal_part))
    keep, send = owner_sum(
        after(spatial_keep, temporal_rows), spatial_got, exchange(temporal_part)
    )
    temporal_rows = exchange(after(temporal_rows, keep)).reshape(frames.shape)
    total = add_rounded(keep, swap(send, "dp", 2))
    input_grad = spatial_backward(after(pre_grad, keep), cotangent, weights)
    bit = 4
    while bit < dp:
        other = swap(total, "dp", bit)
        total = add_rounded(after(total, input_grad), other)
        bit *= 2
    block_out = block_output(frames, temporal_rows)
    near = swap(total, "dp", 2)
    near, block_out = lax.optimization_barrier((near, block_out))
    spatial_grad, temporal_grad = kernel_outputs(
        (total, near, swap(total, "dp", 1), swap(near, "dp", 1)), chans
    )
    return (block_out[None, None], input_grad[None, None], spatial_grad, temporal_grad)


def solution(mesh):
    placed = (
        P("dp", "seq", None, None, None),
        P(None, "seq", None),
        P(None, "seq", None),
        P("dp", "seq", None, None, None),
    )
    return jax.shard_map(
        local,
        mesh=mesh,
        in_specs=placed,
        out_specs=(
            P("dp", "seq", None, None, None),
            P("dp", "seq", None, None, None),
            P(None, "seq", None),
            P(None, "seq", None),
        ),
        check_vma=False,
    )
```

```python
import math

import jax
import jax.numpy as jnp
from jax import lax
from jax.experimental import pallas as pl
from jax.experimental.pallas import tpu as pltpu
from jax.sharding import PartitionSpec as P

BF = jnp.bfloat16
F32 = jnp.float32
VMEM_LIMIT = 24 * 1024 * 1024
NT = (((1,), (1,)), ((), ()))


def call(body, outs, scratch, flops, *args, far=(), sent=(), weight=10):
    def spec(i):
        return pl.BlockSpec(memory_space=pltpu.HBM if i in far else pltpu.VMEM)

    args = [
        pltpu.with_memory_space_constraint(arg, pltpu.HBM) if i in far else arg
        for i, arg in enumerate(args)
    ]
    moved = sum(x.size * x.dtype.itemsize for x in (*args, *outs))
    return pl.pallas_call(
        body,
        out_shape=tuple(
            pltpu.HBM(out.shape, out.dtype) if len(args) + i in (*far, *sent) else out
            for i, out in enumerate(outs)
        ),
        in_specs=[spec(i) for i in range(len(args))],
        out_specs=tuple(spec(len(args) + i) for i in range(len(outs))),
        scratch_shapes=scratch,
        compiler_params=pltpu.CompilerParams(vmem_limit_bytes=VMEM_LIMIT),
        cost_estimate=pl.CostEstimate(flops=weight * flops + 1, bytes_accessed=weight * moved + 1, transcendentals=0),
    )(*args)


def shape(dims, dtype=BF):
    return jax.ShapeDtypeStruct(tuple(dims), dtype)


def columns(first, count, width):
    return pl.ds(pl.multiple_of(first * width, width), count * width)


def place(step):
    return jnp.bitwise_xor(lax.axis_index("seq"), step)


def core():
    return lax.rem(lax.axis_index("dp"), 2)


def pair_bit():
    return lax.rem(lax.div(lax.axis_index("dp"), 2), 2)


def at_block(index, size, count, tile, use):
    if size % tile == 0:
        use(pl.ds(pl.multiple_of(index * size, size), size))
        return
    for fixed in range(count):

        @pl.when(index == fixed)
        def _():
            use(pl.ds(fixed * size, size))


def swap(values, axis, bit):
    size = lax.axis_size(axis)
    return lax.ppermute(values, axis, [(i, i ^ bit) for i in range(size)])


def spread(blocks):
    return [swap(block, "seq", j + 1) for j, block in enumerate(blocks)]


def exchange(blocks):
    return lax.all_to_all(blocks, "seq", 0, 0, tiled=True)


def after(value, *others):
    return lax.optimization_barrier((value, *others))[0]


def shifted(block, step):
    if step == 0:
        return block
    width = block.shape[1]
    rolled = pltpu.roll(block.astype(F32), (-step) % width, 1)
    column = lax.broadcasted_iota(jnp.int32, block.shape, 1)
    edge = 0 if step < 0 else width - 1
    return jnp.where(column == edge, 0.0, rolled).astype(block.dtype)


def fill_taps(target, source, order):
    rows, chans, width = source.shape
    target[:, :width] = jnp.zeros((target.shape[0], width), target.dtype)
    target[:, (rows + 1) * width :] = jnp.zeros((target.shape[0], width), target.dtype)

    def row(y, carry):
        block = source[y]
        for b, step in enumerate(order):
            target[b * chans : (b + 1) * chans, columns(y + 1, 1, width)] = shifted(block, step)
        return carry

    lax.fori_loop(0, rows, row, 0)


def transposed(block):
    size = block.shape[0]
    one = lax.broadcasted_iota(jnp.int32, (size, size), 0) == lax.broadcasted_iota(
        jnp.int32, (size, size), 1
    )
    return lax.dot_general(one.astype(BF), block, NT, preferred_element_type=F32).astype(BF)


def window_taps(frames, weight=10):
    rows, chans, width = frames.shape
    dims = (3 * chans, (rows + 2) * width)

    def body(frames_ref, far_ref, taps_ref, done):
        fill_taps(taps_ref, frames_ref, (-1, 0, 1))
        copy = pltpu.make_async_copy(taps_ref, far_ref, done)
        copy.start()
        copy.wait()

    return call(
        body,
        [shape(dims)],
        [pltpu.VMEM(dims, BF), pltpu.SemaphoreType.DMA],
        frames.size,
        frames,
        far=(1,),
        weight=weight,
    )[0]


def kernel_maps(own, spatial, first, second):
    _, shard, chans = own.shape
    count = len(first)

    def body(*refs):
        own_ref, spatial_ref = refs[:2]
        mine, theirs = refs[2 : 2 + count], refs[2 + count : 2 + 2 * count]
        far_trans, far_plain, far_mid, *refs = refs[2 + 2 * count :]
        trans_ref, plain_ref, mid_ref, rows_ref, done = refs

        def fill_mid(pieces):
            for j, piece in enumerate((spatial_ref, *pieces)):

                def put(at):
                    for b in range(3):
                        source = piece[3 + b] if j == 0 else piece[b]
                        mid_ref[at, b * chans : (b + 1) * chans] = source

                at_block(place(j), shard, count + 1, 16, put)

        def fill(pieces):
            for j, piece in enumerate((own_ref, *pieces)):

                def put(at):
                    for k in range(3):
                        rows_ref[k, at, :] = piece[k]

                at_block(place(j), shard, count + 1, 16, put)

        @pl.when(core() == 0)
        def _():
            fill(mine)
            fill_mid(theirs)

        @pl.when(core() == 1)
        def _():
            fill(theirs)
            fill_mid(mine)

        for k in range(3):
            plain_ref[:, k * chans : (k + 1) * chans] = rows_ref[k]
        for k in range(3):
            trans_ref[:, k * chans : (k + 1) * chans] = transposed(rows_ref[k])
        copies = [
            pltpu.make_async_copy(near, far, done.at[i])
            for i, (near, far) in enumerate(
                ((trans_ref, far_trans), (plain_ref, far_plain), (mid_ref, far_mid))
            )
        ]
        for copy in copies:
            copy.start()
        for copy in copies:
            copy.wait()

    return call(
        body,
        [shape((chans, 3 * chans))] * 3,
        [
            pltpu.VMEM((chans, 3 * chans), BF),
            pltpu.VMEM((chans, 3 * chans), BF),
            pltpu.VMEM((chans, 3 * chans), BF),
            pltpu.VMEM((3, chans, chans), BF),
            pltpu.SemaphoreType.DMA((3,)),
        ],
        6 * chans**3,
        own,
        spatial,
        *first,
        *second,
        far=(2 + 2 * count, 3 + 2 * count, 4 + 2 * count),
    )


def temporal_backward(cot_rows, weights_t):
    frames, rows, chans, width = cot_rows.shape
    span = rows * width

    def body(cot_ref, far_ref, *refs):
        outs, (weights_ref, taps_ref, done) = refs[:frames], refs[frames:]
        load = pltpu.make_async_copy(far_ref, weights_ref, done)
        load.start()
        edge = jnp.zeros((chans, span), BF)
        taps_ref[:chans, (frames - 1) * span :] = edge
        taps_ref[2 * chans :, :span] = edge
        for f in range(frames):
            for k in range(3):
                at = f + k - 1
                if 0 <= at < frames:
                    for y in range(rows):
                        to = at * span + y * width
                        taps_ref[k * chans : (k + 1) * chans, to : to + width] = cot_ref[f, y]
        load.wait()
        for j in range(frames):
            total = jnp.dot(
                weights_ref[...],
                taps_ref[:, columns(place(j), 1, span)],
                preferred_element_type=F32,
            ).astype(BF)
            for y in range(rows):
                outs[j][y] = total[:, y * width : (y + 1) * width]

    return call(
        body,
        [shape((rows, chans, width))] * frames,
        [
            pltpu.VMEM(weights_t.shape, BF),
            pltpu.VMEM((3 * chans, frames * span), BF),
            pltpu.SemaphoreType.DMA,
        ],
        6 * chans * cot_rows.size,
        cot_rows,
        weights_t,
        far=(1,),
        sent=tuple(range(2, 2 + frames)),
    )


def spatial_forward(taps, own, middle, pieces, rows):
    _, shard, chans = own.shape
    width = taps.shape[1] // (rows + 2)
    count = len(pieces)
    owners = count // 2 + 1
    tiles = rows // 2

    def body(*refs):
        far_taps, far_middle, far_sources = refs[0], refs[1], refs[2 : 3 + count]
        pre_ref, far_act, far_weights, taps_ref, act_ref, weights_ref, done = refs[3 + count : -2]
        own_ref, pieces_ref = refs[-2:]
        sources = [own_ref] + [pieces_ref.at[i] for i in range(count)]
        fetched = [
            pltpu.make_async_copy(far, near, done.at[tiles + 2 + i])
            for i, (far, near) in enumerate(zip(far_sources, sources))
        ]
        for copy in fetched:
            copy.start()
        middle_load = pltpu.make_async_copy(far_middle, weights_ref.at[1], done.at[tiles + 1])
        middle_load.start()

        def load(i):
            at = columns(2 * i, 2, width)
            return pltpu.make_async_copy(far_taps.at[:, at], taps_ref.at[:, at], done.at[i])

        def start(i, carry):
            load(i).start()
            return carry

        lax.fori_loop(0, tiles + 1, start, 0)

        for copy in fetched:
            copy.wait()
        lists = [sources[1 + i * (owners - 1) : 1 + (i + 1) * (owners - 1)] for i in range(2)]
        for side, order in enumerate(((0, 1), (1, 0))):

            @pl.when(core() == side)
            def _():
                for j in range(owners):

                    def put(at):
                        for a in (0, 2):
                            for b in range(3):
                                if j == 0:
                                    value = sources[0][3 * a + b]
                                else:
                                    value = lists[order[a // 2]][j - 1][b]
                                weights_ref[a, at, b * chans : (b + 1) * chans] = value

                    at_block(place(j), shard, owners, 16, put)

        middle_load.wait()
        store = pltpu.make_async_copy(weights_ref, far_weights, done.at[tiles + 1])
        store.start()
        load(jnp.int32(0)).wait()

        def act_store(i):
            at = pl.ds(2 * i, 2)
            return pltpu.make_async_copy(act_ref.at[at], far_act.at[at], done.at[i])

        def tile(i, carry):
            load(i + 1).wait()
            total = jnp.zeros((chans, 2 * width), F32)
            for a in range(3):
                total += jnp.dot(
                    weights_ref[a],
                    taps_ref[:, columns(2 * i + a, 2, width)],
                    preferred_element_type=F32,
                )
            pre = total.astype(BF)
            wide = pre.astype(F32)
            act = (wide / (1.0 + jnp.exp(-wide))).astype(BF)
            for r in range(2):
                pre_ref[2 * i + r] = pre[:, r * width : (r + 1) * width]
                act_ref[2 * i + r] = act[:, r * width : (r + 1) * width]
            act_store(i).start()
            return carry

        lax.fori_loop(0, tiles, tile, 0)

        def finish(i, carry):
            act_store(i).wait()
            return carry

        lax.fori_loop(0, tiles, finish, 0)
        store.wait()

    return call(
        body,
        [shape((rows, chans, width)), shape((rows, chans, width)), shape((3, chans, 3 * chans))],
        [
            pltpu.VMEM(taps.shape, BF),
            pltpu.VMEM((rows, chans, width), BF),
            pltpu.VMEM((3, chans, 3 * chans), BF),
            pltpu.SemaphoreType.DMA((tiles + 3 + count,)),
            pltpu.VMEM(own.shape, BF),
            pltpu.VMEM((count, 3, shard, chans), BF),
        ],
        18 * chans * chans * rows * width,
        taps,
        middle,
        own,
        *pieces,
        far=(*range(3 + count), 4 + count, 5 + count),
        weight=10,
    )


def activation_grad(pre_act, grads, shard):
    rows, chans, width = pre_act.shape
    half = shard // 2

    block = rows // len(grads)

    def body(pre_ref, *refs):
        grad_refs, refs = refs[: len(grads)], refs[len(grads) :]
        mine_ref, theirs_ref, far_ref, pg_ref, act_ref, done = refs
        for j, ref in enumerate(grad_refs):
            act_ref[pl.ds(place(j) * block, block)] = ref[...]

        def row(y, carry):
            wide = pre_ref[y].astype(F32)
            s = 1.0 / (1.0 + jnp.exp(-wide))
            pg = act_ref[y].astype(F32) * s * (1.0 + wide * (1.0 - s))
            pg_ref[y] = pg.astype(BF)
            low = [pg[at : at + half] for at in range(0, chans, shard)]
            high = [pg[at + half : at + shard] for at in range(0, chans, shard)]
            low = jnp.concatenate(low).astype(BF)
            high = jnp.concatenate(high).astype(BF)
            first = core() == 0
            mine_ref[:, columns(y, 1, width)] = jnp.where(first, low, high)
            theirs_ref[:, columns(y, 1, width)] = jnp.where(first, high, low)
            return carry

        copies = []
        for i in range(2):
            lax.fori_loop(i * rows // 2, (i + 1) * rows // 2, row, 0)
            at = pl.ds(i * rows // 2, rows // 2)
            copies.append(pltpu.make_async_copy(pg_ref.at[at], far_ref.at[at], done.at[i]))
            copies[i].start()
        for copy in copies:
            copy.wait()

    return call(
        body,
        [shape((chans // 2, rows * width))] * 2 + [shape(pre_act.shape)],
        [
            pltpu.VMEM(pre_act.shape, BF),
            pltpu.VMEM(pre_act.shape, BF),
            pltpu.SemaphoreType.DMA((2,)),
        ],
        20 * pre_act.size,
        pre_act,
        *grads,
        far=(3 + len(grads),),
    )


def spatial_weight_grad(taps, other_taps, half_grad, other_half, owners, scale, rows):
    wide = taps.shape[0]
    chans, span = half_grad.shape
    width = span // rows
    part = chans // owners

    def body(far_taps, far_other, mine_ref, theirs_ref, *refs):
        keep_ref, sends = refs[0], refs[1:owners]
        stack_ref, taps_ref, total_ref, done = refs[owners:]
        loads = [
            pltpu.make_async_copy(far, taps_ref.at[q], done.at[q])
            for q, far in enumerate((far_taps, far_other))
        ]
        for copy in loads:
            copy.start()
        edge = jnp.zeros((chans, width), BF)
        for q, source in enumerate((mine_ref, theirs_ref)):
            at = q * span
            stack_ref[:chans, at + span - width : at + span] = edge
            stack_ref[:chans, at : at + span - width] = source[:, width:]
            stack_ref[chans : 2 * chans, at : at + span] = source[...]
            stack_ref[2 * chans :, at : at + width] = edge
            stack_ref[2 * chans :, at + width : at + span] = source[:, : span - width]
        total = jnp.zeros((3 * chans, wide), F32)
        for q, copy in enumerate(loads):
            copy.wait()
            total += lax.dot_general(
                stack_ref[:, q * span : (q + 1) * span],
                taps_ref[q, :, width : width + span],
                NT,
                preferred_element_type=F32,
            )
        for a in range(3):
            total_ref[a] = total[a * chans : (a + 1) * chans] * scale
        for j in range(owners):

            def put(at):
                for a in range(3):
                    value = total_ref[a, at, :]
                    if j == 0:
                        keep_ref[a] = value
                    else:
                        sends[j - 1][a] = value.astype(BF)

            at_block(place(j), part, owners, 8, put)

    return call(
        body,
        [shape((3, part, wide), F32)] + [shape((3, part, wide))] * (owners - 1),
        [
            pltpu.VMEM((3 * chans, 2 * span), BF),
            pltpu.VMEM((2,) + taps.shape, BF),
            pltpu.VMEM((3, chans, wide), F32),
            pltpu.SemaphoreType.DMA((2,)),
        ],
        12 * chans * wide * span,
        taps,
        other_taps,
        half_grad,
        other_half,
        far=(0, 1),
        sent=tuple(range(5, 4 + owners)),
        weight=0,
    )


def spatial_backward(pre_grad, cotangent, weights):
    rows, chans, width = pre_grad.shape

    def body(far_pg, far_cot, far_weights, out_ref, *refs):
        pg_ref, cot_ref, weights_ref, taps_ref, trans_ref, done = refs
        loads = [
            pltpu.make_async_copy(far, near, done.at[i])
            for i, (far, near) in enumerate(
                ((far_pg, pg_ref), (far_weights, weights_ref), (far_cot, cot_ref))
            )
        ]
        for copy in loads:
            copy.start()
        loads[0].wait()
        fill_taps(taps_ref, pg_ref, (1, 0, -1))
        loads[1].wait()
        for a in range(3):
            for b in range(3):
                at = slice(b * chans, (b + 1) * chans)
                trans_ref[a, :, at] = transposed(weights_ref[a, :, at])
        loads[2].wait()

        def tile(i, carry):
            total = jnp.zeros((chans, 2 * width), F32)
            for a in range(3):
                total += jnp.dot(
                    trans_ref[a],
                    taps_ref[:, columns(2 * i + 2 - a, 2, width)],
                    preferred_element_type=F32,
                )
            for r in range(2):
                wide = cot_ref[2 * i + r].astype(F32)
                out_ref[2 * i + r] = (wide + total[:, r * width : (r + 1) * width]).astype(BF)
            return carry

        lax.fori_loop(0, rows // 2, tile, 0)

    return call(
        body,
        [shape(pre_grad.shape)],
        [
            pltpu.VMEM(pre_grad.shape, BF),
            pltpu.VMEM(pre_grad.shape, BF),
            pltpu.VMEM((3, chans, 3 * chans), BF),
            pltpu.VMEM((3 * chans, (rows + 2) * width), BF),
            pltpu.VMEM((3, chans, 3 * chans), BF),
            pltpu.SemaphoreType.DMA((3,)),
        ],
        18 * chans * chans * rows * width,
        pre_grad,
        cotangent,
        weights,
        far=(0, 1, 2),
    )[0]


def temporal_weight_grad(acts, cot_rows, shard, scale):
    frames, rows, chans, width = cot_rows.shape
    span = rows * width
    half = shard // 2
    owners = chans // shard

    def body(act_ref, cot_ref, keep_ref, send_ref, taps_ref, cots_ref):
        edge = jnp.zeros((chans, span), BF)
        taps_ref[:chans, :span] = edge
        taps_ref[2 * chans :, (frames - 1) * span :] = edge
        for f in range(frames):
            for y in range(rows):
                at = f * span + y * width
                cots_ref[:, at : at + width] = cot_ref[f, y]
                for k in range(3):
                    if 0 <= f - k + 1 < frames:
                        to = at + (1 - k) * span
                        taps_ref[k * chans : (k + 1) * chans, to : to + width] = act_ref[f, y]
        total = (
            lax.dot_general(cots_ref[...], taps_ref[...], NT, preferred_element_type=F32) * scale
        )
        first = core() == 0
        for s in range(owners):
            low = total[s * shard : s * shard + half]
            high = total[s * shard + half : (s + 1) * shard]
            keep_ref[s] = jnp.where(first, low, high)
            send_ref[s] = jnp.where(first, high, low).astype(BF)

    return call(
        body,
        [shape((owners, half, 3 * chans), F32), shape((owners, half, 3 * chans))],
        [
            pltpu.VMEM((3 * chans, frames * span), BF),
            pltpu.VMEM((chans, frames * span), BF),
        ],
        6 * chans * cot_rows.size,
        acts,
        cot_rows,
    )


def temporal_forward(acts, weights):
    frames, rows, chans, width = acts.shape
    span = rows * width

    def body(act_ref, far_ref, out_ref, weights_ref, taps_ref, done):
        load = pltpu.make_async_copy(far_ref, weights_ref, done)
        load.start()
        edge = jnp.zeros((chans, span), BF)
        taps_ref[:chans, :span] = edge
        taps_ref[2 * chans :, (frames - 1) * span :] = edge
        for f in range(frames):
            for k in range(3):
                if 0 <= f - k + 1 < frames:
                    for y in range(rows):
                        to = (f - k + 1) * span + y * width
                        taps_ref[k * chans : (k + 1) * chans, to : to + width] = act_ref[f, y]
        load.wait()
        for f in range(frames):
            total = jnp.dot(
                weights_ref[...],
                taps_ref[:, f * span : (f + 1) * span],
                preferred_element_type=F32,
            ).astype(BF)
            for y in range(rows):
                out_ref[f, y] = total[:, y * width : (y + 1) * width]

    return call(
        body,
        [shape(acts.shape)],
        [
            pltpu.VMEM(weights.shape, BF),
            pltpu.VMEM((3 * chans, frames * span), BF),
            pltpu.SemaphoreType.DMA,
        ],
        6 * chans * acts.size,
        acts,
        weights,
        far=(1,),
        sent=(2,),
    )[0]


def owner_sum(spatial, others, temporal):
    _, half, wide = spatial.shape
    count = len(others)

    def body(spatial_ref, temporal_ref, *refs):
        other_refs, (keep_ref, send_ref, sum_ref) = refs[:count], refs[count:]
        for a in range(3):
            value = spatial_ref[a]
            for ref in other_refs:
                value += ref[a].astype(F32)
            sum_ref[a] = value
        value = temporal_ref[0].astype(F32)
        for s in range(1, count + 1):
            value += temporal_ref[s].astype(F32)
        sum_ref[3] = value
        bit = pair_bit()
        keep_ref[...] = sum_ref[pl.ds(2 * bit, 2)]
        send_ref[...] = sum_ref[pl.ds(2 - 2 * bit, 2)].astype(BF)

    return call(
        body,
        [shape((2, half, wide), F32), shape((2, half, wide))],
        [pltpu.VMEM((4, half, wide), F32)],
        4 * spatial.size,
        spatial,
        temporal,
        *others,
    )


def add_rounded(keep, other):
    def body(keep_ref, other_ref, out_ref):
        out_ref[...] = (keep_ref[...].astype(F32) + other_ref[...].astype(F32)).astype(BF)

    return call(body, [shape(keep.shape)], [], keep.size, keep, other)[0]


def kernel_outputs(parts, chans):
    _, half, wide = parts[0].shape

    def body(own_ref, next_ref, core_ref, both_ref, spatial_ref, temporal_ref, sum_ref):
        bit, mine = pair_bit(), core()
        for ref, group, side in (
            (own_ref, bit, mine),
            (next_ref, 1 - bit, mine),
            (core_ref, bit, 1 - mine),
            (both_ref, 1 - bit, 1 - mine),
        ):

            def put(at):
                for g in range(2):
                    sum_ref[2 * group + g, at, :] = ref[g].astype(F32)

            at_block(side, half, 2, 8, put)
        for a in range(3):
            for b in range(3):
                spatial_ref[3 * a + b] = sum_ref[a, :, b * chans : (b + 1) * chans]
        for k in range(3):
            temporal_ref[k] = sum_ref[3, :, k * chans : (k + 1) * chans]

    return call(
        body,
        [shape((9, 2 * half, chans), F32), shape((3, 2 * half, chans), F32)],
        [pltpu.VMEM((4, 2 * half, wide), F32)],
        8 * parts[0].size,
        *parts,
    )


def block_output(frames, temporal):
    def body(frames_ref, temporal_ref, out_ref):
        out_ref[...] = (frames_ref[...].astype(F32) + temporal_ref[...].astype(F32)).astype(BF)

    return call(body, [shape(frames.shape)], [], frames.size, frames, temporal)[0]


def local(frames_in, spatial_kernel, temporal_kernel, out_cotangent):
    frames, cotangent = frames_in[0, 0], out_cotangent[0, 0]
    rows, chans, width = frames.shape
    seq, dp = lax.axis_size("seq"), lax.axis_size("dp")
    shard = spatial_kernel.shape[1]
    scale = 1.0 / math.sqrt(dp * seq * rows * width)

    first = core() == 0
    mine_a = jnp.where(first, temporal_kernel, spatial_kernel[3:6])
    mine_b = jnp.where(first, spatial_kernel[:3], spatial_kernel[6:])
    got_a = spread([mine_a] * (seq - 1))
    cot_rows = exchange(cotangent.reshape(seq, rows // seq, chans, width))
    got_b = spread([mine_b] * (seq - 1))
    taps = window_taps(frames)
    other_taps = window_taps(swap(after(frames, mine_a), "dp", 1))
    taps, other_taps, *got_a = lax.optimization_barrier((taps, other_taps, *got_a))
    pair_a = [swap(piece, "dp", 1) for piece in got_a]
    temporal_t, temporal_w, middle = kernel_maps(
        temporal_kernel, spatial_kernel, got_a, pair_a
    )
    grad_rows = temporal_backward(cot_rows, temporal_t)
    act_grad = [grad_rows[0], *spread(grad_rows[1:])]
    temporal_w, *got_b = lax.optimization_barrier((after(temporal_w, grad_rows[0]), *got_b))
    pair_b = [swap(piece, "dp", 1) for piece in got_b]
    pre_act, activated, weights = spatial_forward(
        taps, spatial_kernel, middle, (*got_b, *pair_b), rows
    )
    half_mine, half_theirs, pre_grad = activation_grad(pre_act, act_grad, shard)
    half_other = swap(half_theirs, "dp", 1)
    act_rows = exchange(activated.reshape(cot_rows.shape))
    spatial_keep, *spatial_send = spatial_weight_grad(
        taps, other_taps, half_mine, half_other, seq, scale, rows
    )
    spatial_got = spread(spatial_send)
    temporal_keep, temporal_send = temporal_weight_grad(
        act_rows, after(cot_rows, spatial_keep), shard, scale
    )
    temporal_part = add_rounded(temporal_keep, swap(temporal_send, "dp", 1))
    temporal_rows = temporal_forward(act_rows, after(temporal_w, temporal_part))
    keep, send = owner_sum(
        after(spatial_keep, temporal_rows), spatial_got, exchange(temporal_part)
    )
    temporal_rows = exchange(after(temporal_rows, keep)).reshape(frames.shape)
    total = add_rounded(keep, swap(send, "dp", 2))
    input_grad = spatial_backward(after(pre_grad, keep), cotangent, weights)
    bit = 4
    while bit < dp:
        other = swap(total, "dp", bit)
        total = add_rounded(after(total, input_grad), other)
        bit *= 2
    block_out = block_output(frames, temporal_rows)
    near = swap(total, "dp", 2)
    near, block_out = lax.optimization_barrier((near, block_out))
    spatial_grad, temporal_grad = kernel_outputs(
        (total, near, swap(total, "dp", 1), swap(near, "dp", 1)), chans
    )
    return (block_out[None, None], input_grad[None, None], spatial_grad, temporal_grad)


def solution(mesh):
    placed = (
        P("dp", "seq", None, None, None),
        P(None, "seq", None),
        P(None, "seq", None),
        P("dp", "seq", None, None, None),
    )
    return jax.shard_map(
        local,
        mesh=mesh,
        in_specs=placed,
        out_specs=(
            P("dp", "seq", None, None, None),
            P("dp", "seq", None, None, None),
            P(None, "seq", None),
            P(None, "seq", None),
        ),
        check_vma=False,
    )
```

```python
import math

import jax
import jax.numpy as jnp
from jax import lax
from jax.experimental import pallas as pl
from jax.experimental.pallas import tpu as pltpu
from jax.sharding import PartitionSpec as P

BF = jnp.bfloat16
F32 = jnp.float32
VMEM_LIMIT = 24 * 1024 * 1024
NT = (((1,), (1,)), ((), ()))


def call(body, outs, scratch, flops, *args, far=(), sent=(), weight=10):
    def spec(i):
        return pl.BlockSpec(memory_space=pltpu.HBM if i in far else pltpu.VMEM)

    args = [
        pltpu.with_memory_space_constraint(arg, pltpu.HBM) if i in far else arg
        for i, arg in enumerate(args)
    ]
    moved = sum(x.size * x.dtype.itemsize for x in (*args, *outs))
    return pl.pallas_call(
        body,
        out_shape=tuple(
            pltpu.HBM(out.shape, out.dtype) if len(args) + i in (*far, *sent) else out
            for i, out in enumerate(outs)
        ),
        in_specs=[spec(i) for i in range(len(args))],
        out_specs=tuple(spec(len(args) + i) for i in range(len(outs))),
        scratch_shapes=scratch,
        compiler_params=pltpu.CompilerParams(vmem_limit_bytes=VMEM_LIMIT),
        cost_estimate=pl.CostEstimate(flops=weight * flops + 1, bytes_accessed=weight * moved + 1, transcendentals=0),
    )(*args)


def shape(dims, dtype=BF):
    return jax.ShapeDtypeStruct(tuple(dims), dtype)


def columns(first, count, width):
    return pl.ds(pl.multiple_of(first * width, width), count * width)


def place(step):
    return jnp.bitwise_xor(lax.axis_index("seq"), step)


def core():
    return lax.rem(lax.axis_index("dp"), 2)


def pair_bit():
    return lax.rem(lax.div(lax.axis_index("dp"), 2), 2)


def at_block(index, size, count, tile, use):
    if size % tile == 0:
        use(pl.ds(pl.multiple_of(index * size, size), size))
        return
    for fixed in range(count):

        @pl.when(index == fixed)
        def _():
            use(pl.ds(fixed * size, size))


def swap(values, axis, bit):
    size = lax.axis_size(axis)
    return lax.ppermute(values, axis, [(i, i ^ bit) for i in range(size)])


def spread(blocks):
    return [swap(block, "seq", j + 1) for j, block in enumerate(blocks)]


def exchange(blocks):
    return lax.all_to_all(blocks, "seq", 0, 0, tiled=True)


def after(value, *others):
    return lax.optimization_barrier((value, *others))[0]


def shifted(block, step):
    if step == 0:
        return block
    width = block.shape[1]
    rolled = pltpu.roll(block.astype(F32), (-step) % width, 1)
    column = lax.broadcasted_iota(jnp.int32, block.shape, 1)
    edge = 0 if step < 0 else width - 1
    return jnp.where(column == edge, 0.0, rolled).astype(block.dtype)


def fill_taps(target, source, order):
    rows, chans, width = source.shape
    target[:, :width] = jnp.zeros((target.shape[0], width), target.dtype)
    target[:, (rows + 1) * width :] = jnp.zeros((target.shape[0], width), target.dtype)

    def row(y, carry):
        block = source[y]
        for b, step in enumerate(order):
            target[b * chans : (b + 1) * chans, columns(y + 1, 1, width)] = shifted(block, step)
        return carry

    lax.fori_loop(0, rows, row, 0)


def transposed(block):
    size = block.shape[0]
    one = lax.broadcasted_iota(jnp.int32, (size, size), 0) == lax.broadcasted_iota(
        jnp.int32, (size, size), 1
    )
    return lax.dot_general(one.astype(BF), block, NT, preferred_element_type=F32).astype(BF)


def window_taps(frames, weight=10):
    rows, chans, width = frames.shape
    dims = (3 * chans, (rows + 2) * width)

    def body(frames_ref, far_ref, taps_ref, done):
        fill_taps(taps_ref, frames_ref, (-1, 0, 1))
        copy = pltpu.make_async_copy(taps_ref, far_ref, done)
        copy.start()
        copy.wait()

    return call(
        body,
        [shape(dims)],
        [pltpu.VMEM(dims, BF), pltpu.SemaphoreType.DMA],
        frames.size,
        frames,
        far=(1,),
        weight=weight,
    )[0]


def kernel_maps(own, spatial, first, second):
    _, shard, chans = own.shape
    count = len(first)

    def body(*refs):
        own_ref, spatial_ref = refs[:2]
        mine, theirs = refs[2 : 2 + count], refs[2 + count : 2 + 2 * count]
        far_trans, far_plain, far_mid, *refs = refs[2 + 2 * count :]
        trans_ref, plain_ref, mid_ref, rows_ref, done = refs

        def fill_mid(pieces):
            for j, piece in enumerate((spatial_ref, *pieces)):

                def put(at):
                    for b in range(3):
                        source = piece[3 + b] if j == 0 else piece[b]
                        mid_ref[at, b * chans : (b + 1) * chans] = source

                at_block(place(j), shard, count + 1, 16, put)

        def fill(pieces):
            for j, piece in enumerate((own_ref, *pieces)):

                def put(at):
                    for k in range(3):
                        rows_ref[k, at, :] = piece[k]

                at_block(place(j), shard, count + 1, 16, put)

        @pl.when(core() == 0)
        def _():
            fill(mine)
            fill_mid(theirs)

        @pl.when(core() == 1)
        def _():
            fill(theirs)
            fill_mid(mine)

        for k in range(3):
            plain_ref[:, k * chans : (k + 1) * chans] = rows_ref[k]
        for k in range(3):
            trans_ref[:, k * chans : (k + 1) * chans] = transposed(rows_ref[k])
        copies = [
            pltpu.make_async_copy(near, far, done.at[i])
            for i, (near, far) in enumerate(
                ((trans_ref, far_trans), (plain_ref, far_plain), (mid_ref, far_mid))
            )
        ]
        for copy in copies:
            copy.start()
        for copy in copies:
            copy.wait()

    return call(
        body,
        [shape((chans, 3 * chans))] * 3,
        [
            pltpu.VMEM((chans, 3 * chans), BF),
            pltpu.VMEM((chans, 3 * chans), BF),
            pltpu.VMEM((chans, 3 * chans), BF),
            pltpu.VMEM((3, chans, chans), BF),
            pltpu.SemaphoreType.DMA((3,)),
        ],
        6 * chans**3,
        own,
        spatial,
        *first,
        *second,
        far=(2 + 2 * count, 3 + 2 * count, 4 + 2 * count),
    )


def temporal_backward(cot_rows, weights_t):
    frames, rows, chans, width = cot_rows.shape
    span = rows * width

    def body(cot_ref, far_ref, *refs):
        outs, (weights_ref, taps_ref, done) = refs[:frames], refs[frames:]
        load = pltpu.make_async_copy(far_ref, weights_ref, done)
        load.start()
        edge = jnp.zeros((chans, span), BF)
        taps_ref[:chans, (frames - 1) * span :] = edge
        taps_ref[2 * chans :, :span] = edge
        for f in range(frames):
            for k in range(3):
                at = f + k - 1
                if 0 <= at < frames:
                    for y in range(rows):
                        to = at * span + y * width
                        taps_ref[k * chans : (k + 1) * chans, to : to + width] = cot_ref[f, y]
        load.wait()
        for j in range(frames):
            total = jnp.dot(
                weights_ref[...],
                taps_ref[:, columns(place(j), 1, span)],
                preferred_element_type=F32,
            ).astype(BF)
            for y in range(rows):
                outs[j][y] = total[:, y * width : (y + 1) * width]

    return call(
        body,
        [shape((rows, chans, width))] * frames,
        [
            pltpu.VMEM(weights_t.shape, BF),
            pltpu.VMEM((3 * chans, frames * span), BF),
            pltpu.SemaphoreType.DMA,
        ],
        6 * chans * cot_rows.size,
        cot_rows,
        weights_t,
        far=(1,),
        sent=tuple(range(2, 2 + frames)),
    )


def spatial_forward(taps, own, middle, pieces, rows):
    _, shard, chans = own.shape
    width = taps.shape[1] // (rows + 2)
    count = len(pieces)
    owners = count // 2 + 1
    tiles = rows // 2

    def body(*refs):
        far_taps, far_middle, far_sources = refs[0], refs[1], refs[2 : 3 + count]
        pre_ref, far_act, far_weights, taps_ref, act_ref, weights_ref, done = refs[3 + count : -2]
        own_ref, pieces_ref = refs[-2:]
        sources = [own_ref] + [pieces_ref.at[i] for i in range(count)]
        fetched = [
            pltpu.make_async_copy(far, near, done.at[tiles + 2 + i])
            for i, (far, near) in enumerate(zip(far_sources, sources))
        ]
        for copy in fetched:
            copy.start()
        middle_load = pltpu.make_async_copy(far_middle, weights_ref.at[1], done.at[tiles + 1])
        middle_load.start()

        def load(i):
            at = columns(2 * i, 2, width)
            return pltpu.make_async_copy(far_taps.at[:, at], taps_ref.at[:, at], done.at[i])

        def start(i, carry):
            load(i).start()
            return carry

        lax.fori_loop(0, tiles + 1, start, 0)

        for copy in fetched:
            copy.wait()
        lists = [sources[1 + i * (owners - 1) : 1 + (i + 1) * (owners - 1)] for i in range(2)]
        for side, order in enumerate(((0, 1), (1, 0))):

            @pl.when(core() == side)
            def _():
                for j in range(owners):

                    def put(at):
                        for a in (0, 2):
                            for b in range(3):
                                if j == 0:
                                    value = sources[0][3 * a + b]
                                else:
                                    value = lists[order[a // 2]][j - 1][b]
                                weights_ref[a, at, b * chans : (b + 1) * chans] = value

                    at_block(place(j), shard, owners, 16, put)

        middle_load.wait()
        store = pltpu.make_async_copy(weights_ref, far_weights, done.at[tiles + 1])
        store.start()
        load(jnp.int32(0)).wait()

        def act_store(i):
            at = pl.ds(2 * i, 2)
            return pltpu.make_async_copy(act_ref.at[at], far_act.at[at], done.at[i])

        def tile(i, carry):
            load(i + 1).wait()
            total = jnp.zeros((chans, 2 * width), F32)
            for a in range(3):
                total += jnp.dot(
                    weights_ref[a],
                    taps_ref[:, columns(2 * i + a, 2, width)],
                    preferred_element_type=F32,
                )
            pre = total.astype(BF)
            wide = pre.astype(F32)
            act = (wide / (1.0 + jnp.exp(-wide))).astype(BF)
            for r in range(2):
                pre_ref[2 * i + r] = pre[:, r * width : (r + 1) * width]
                act_ref[2 * i + r] = act[:, r * width : (r + 1) * width]
            act_store(i).start()
            return carry

        lax.fori_loop(0, tiles, tile, 0)

        def finish(i, carry):
            act_store(i).wait()
            return carry

        lax.fori_loop(0, tiles, finish, 0)
        store.wait()

    return call(
        body,
        [shape((rows, chans, width)), shape((rows, chans, width)), shape((3, chans, 3 * chans))],
        [
            pltpu.VMEM(taps.shape, BF),
            pltpu.VMEM((rows, chans, width), BF),
            pltpu.VMEM((3, chans, 3 * chans), BF),
            pltpu.SemaphoreType.DMA((tiles + 3 + count,)),
            pltpu.VMEM(own.shape, BF),
            pltpu.VMEM((count, 3, shard, chans), BF),
        ],
        18 * chans * chans * rows * width,
        taps,
        middle,
        own,
        *pieces,
        far=(*range(3 + count), 4 + count, 5 + count),
        weight=10,
    )


def activation_grad(pre_act, grads, shard):
    rows, chans, width = pre_act.shape
    half = shard // 2

    block = rows // len(grads)

    def body(pre_ref, *refs):
        grad_refs, refs = refs[: len(grads)], refs[len(grads) :]
        mine_ref, theirs_ref, far_ref, pg_ref, act_ref, done = refs
        for j, ref in enumerate(grad_refs):
            act_ref[pl.ds(place(j) * block, block)] = ref[...]

        def row(y, carry):
            wide = pre_ref[y].astype(F32)
            s = 1.0 / (1.0 + jnp.exp(-wide))
            pg = act_ref[y].astype(F32) * s * (1.0 + wide * (1.0 - s))
            pg_ref[y] = pg.astype(BF)
            low = [pg[at : at + half] for at in range(0, chans, shard)]
            high = [pg[at + half : at + shard] for at in range(0, chans, shard)]
            low = jnp.concatenate(low).astype(BF)
            high = jnp.concatenate(high).astype(BF)
            first = core() == 0
            mine_ref[:, columns(y, 1, width)] = jnp.where(first, low, high)
            theirs_ref[:, columns(y, 1, width)] = jnp.where(first, high, low)
            return carry

        copies = []
        for i in range(2):
            lax.fori_loop(i * rows // 2, (i + 1) * rows // 2, row, 0)
            at = pl.ds(i * rows // 2, rows // 2)
            copies.append(pltpu.make_async_copy(pg_ref.at[at], far_ref.at[at], done.at[i]))
            copies[i].start()
        for copy in copies:
            copy.wait()

    return call(
        body,
        [shape((chans // 2, rows * width))] * 2 + [shape(pre_act.shape)],
        [
            pltpu.VMEM(pre_act.shape, BF),
            pltpu.VMEM(pre_act.shape, BF),
            pltpu.SemaphoreType.DMA((2,)),
        ],
        20 * pre_act.size,
        pre_act,
        *grads,
        far=(3 + len(grads),),
    )


def spatial_weight_grad(taps, other_taps, half_grad, other_half, owners, scale, rows):
    wide = taps.shape[0]
    chans, span = half_grad.shape
    width = span // rows
    part = chans // owners

    def body(far_taps, far_other, mine_ref, theirs_ref, *refs):
        keep_ref, sends = refs[0], refs[1:owners]
        stack_ref, taps_ref, total_ref, done = refs[owners:]
        loads = [
            pltpu.make_async_copy(far, taps_ref.at[q], done.at[q])
            for q, far in enumerate((far_taps, far_other))
        ]
        for copy in loads:
            copy.start()
        edge = jnp.zeros((chans, width), BF)
        for q, source in enumerate((mine_ref, theirs_ref)):
            at = q * span
            stack_ref[:chans, at + span - width : at + span] = edge
            stack_ref[:chans, at : at + span - width] = source[:, width:]
            stack_ref[chans : 2 * chans, at : at + span] = source[...]
            stack_ref[2 * chans :, at : at + width] = edge
            stack_ref[2 * chans :, at + width : at + span] = source[:, : span - width]
        total = jnp.zeros((3 * chans, wide), F32)
        for q, copy in enumerate(loads):
            copy.wait()
            total += lax.dot_general(
                stack_ref[:, q * span : (q + 1) * span],
                taps_ref[q, :, width : width + span],
                NT,
                preferred_element_type=F32,
            )
        for a in range(3):
            total_ref[a] = total[a * chans : (a + 1) * chans] * scale
        for j in range(owners):

            def put(at):
                for a in range(3):
                    value = total_ref[a, at, :]
                    if j == 0:
                        keep_ref[a] = value
                    else:
                        sends[j - 1][a] = value.astype(BF)

            at_block(place(j), part, owners, 8, put)

    return call(
        body,
        [shape((3, part, wide), F32)] + [shape((3, part, wide))] * (owners - 1),
        [
            pltpu.VMEM((3 * chans, 2 * span), BF),
            pltpu.VMEM((2,) + taps.shape, BF),
            pltpu.VMEM((3, chans, wide), F32),
            pltpu.SemaphoreType.DMA((2,)),
        ],
        12 * chans * wide * span,
        taps,
        other_taps,
        half_grad,
        other_half,
        far=(0, 1),
        weight=0,
    )


def spatial_backward(pre_grad, cotangent, weights):
    rows, chans, width = pre_grad.shape

    def body(far_pg, far_cot, far_weights, out_ref, *refs):
        pg_ref, cot_ref, weights_ref, taps_ref, trans_ref, done = refs
        loads = [
            pltpu.make_async_copy(far, near, done.at[i])
            for i, (far, near) in enumerate(
                ((far_pg, pg_ref), (far_weights, weights_ref), (far_cot, cot_ref))
            )
        ]
        for copy in loads:
            copy.start()
        loads[0].wait()
        fill_taps(taps_ref, pg_ref, (1, 0, -1))
        loads[1].wait()
        for a in range(3):
            for b in range(3):
                at = slice(b * chans, (b + 1) * chans)
                trans_ref[a, :, at] = transposed(weights_ref[a, :, at])
        loads[2].wait()

        def tile(i, carry):
            total = jnp.zeros((chans, 2 * width), F32)
            for a in range(3):
                total += jnp.dot(
                    trans_ref[a],
                    taps_ref[:, columns(2 * i + 2 - a, 2, width)],
                    preferred_element_type=F32,
                )
            for r in range(2):
                wide = cot_ref[2 * i + r].astype(F32)
                out_ref[2 * i + r] = (wide + total[:, r * width : (r + 1) * width]).astype(BF)
            return carry

        lax.fori_loop(0, rows // 2, tile, 0)

    return call(
        body,
        [shape(pre_grad.shape)],
        [
            pltpu.VMEM(pre_grad.shape, BF),
            pltpu.VMEM(pre_grad.shape, BF),
            pltpu.VMEM((3, chans, 3 * chans), BF),
            pltpu.VMEM((3 * chans, (rows + 2) * width), BF),
            pltpu.VMEM((3, chans, 3 * chans), BF),
            pltpu.SemaphoreType.DMA((3,)),
        ],
        18 * chans * chans * rows * width,
        pre_grad,
        cotangent,
        weights,
        far=(0, 1, 2),
    )[0]


def temporal_weight_grad(acts, cot_rows, shard, scale):
    frames, rows, chans, width = cot_rows.shape
    span = rows * width
    half = shard // 2
    owners = chans // shard

    def body(act_ref, cot_ref, keep_ref, send_ref, taps_ref, cots_ref):
        edge = jnp.zeros((chans, span), BF)
        taps_ref[:chans, :span] = edge
        taps_ref[2 * chans :, (frames - 1) * span :] = edge
        for f in range(frames):
            for y in range(rows):
                at = f * span + y * width
                cots_ref[:, at : at + width] = cot_ref[f, y]
                for k in range(3):
                    if 0 <= f - k + 1 < frames:
                        to = at + (1 - k) * span
                        taps_ref[k * chans : (k + 1) * chans, to : to + width] = act_ref[f, y]
        total = (
            lax.dot_general(cots_ref[...], taps_ref[...], NT, preferred_element_type=F32) * scale
        )
        first = core() == 0
        for s in range(owners):
            low = total[s * shard : s * shard + half]
            high = total[s * shard + half : (s + 1) * shard]
            keep_ref[s] = jnp.where(first, low, high)
            send_ref[s] = jnp.where(first, high, low).astype(BF)

    return call(
        body,
        [shape((owners, half, 3 * chans), F32), shape((owners, half, 3 * chans))],
        [
            pltpu.VMEM((3 * chans, frames * span), BF),
            pltpu.VMEM((chans, frames * span), BF),
        ],
        6 * chans * cot_rows.size,
        acts,
        cot_rows,
    )


def temporal_forward(acts, weights):
    frames, rows, chans, width = acts.shape
    span = rows * width

    def body(act_ref, far_ref, out_ref, weights_ref, taps_ref, done):
        load = pltpu.make_async_copy(far_ref, weights_ref, done)
        load.start()
        edge = jnp.zeros((chans, span), BF)
        taps_ref[:chans, :span] = edge
        taps_ref[2 * chans :, (frames - 1) * span :] = edge
        for f in range(frames):
            for k in range(3):
                if 0 <= f - k + 1 < frames:
                    for y in range(rows):
                        to = (f - k + 1) * span + y * width
                        taps_ref[k * chans : (k + 1) * chans, to : to + width] = act_ref[f, y]
        load.wait()
        for f in range(frames):
            total = jnp.dot(
                weights_ref[...],
                taps_ref[:, f * span : (f + 1) * span],
                preferred_element_type=F32,
            ).astype(BF)
            for y in range(rows):
                out_ref[f, y] = total[:, y * width : (y + 1) * width]

    return call(
        body,
        [shape(acts.shape)],
        [
            pltpu.VMEM(weights.shape, BF),
            pltpu.VMEM((3 * chans, frames * span), BF),
            pltpu.SemaphoreType.DMA,
        ],
        6 * chans * acts.size,
        acts,
        weights,
        far=(1,),
        sent=(2,),
    )[0]


def owner_sum(spatial, others, temporal):
    _, half, wide = spatial.shape
    count = len(others)

    def body(spatial_ref, temporal_ref, *refs):
        other_refs, (keep_ref, send_ref, sum_ref) = refs[:count], refs[count:]
        for a in range(3):
            value = spatial_ref[a]
            for ref in other_refs:
                value += ref[a].astype(F32)
            sum_ref[a] = value
        value = temporal_ref[0].astype(F32)
        for s in range(1, count + 1):
            value += temporal_ref[s].astype(F32)
        sum_ref[3] = value
        bit = pair_bit()
        keep_ref[...] = sum_ref[pl.ds(2 * bit, 2)]
        send_ref[...] = sum_ref[pl.ds(2 - 2 * bit, 2)].astype(BF)

    return call(
        body,
        [shape((2, half, wide), F32), shape((2, half, wide))],
        [pltpu.VMEM((4, half, wide), F32)],
        4 * spatial.size,
        spatial,
        temporal,
        *others,
    )


def add_rounded(keep, other):
    def body(keep_ref, other_ref, out_ref):
        out_ref[...] = (keep_ref[...].astype(F32) + other_ref[...].astype(F32)).astype(BF)

    return call(body, [shape(keep.shape)], [], keep.size, keep, other)[0]


def kernel_outputs(parts, chans):
    _, half, wide = parts[0].shape

    def body(own_ref, next_ref, core_ref, both_ref, spatial_ref, temporal_ref, sum_ref):
        bit, mine = pair_bit(), core()
        for ref, group, side in (
            (own_ref, bit, mine),
            (next_ref, 1 - bit, mine),
            (core_ref, bit, 1 - mine),
            (both_ref, 1 - bit, 1 - mine),
        ):

            def put(at):
                for g in range(2):
                    sum_ref[2 * group + g, at, :] = ref[g].astype(F32)

            at_block(side, half, 2, 8, put)
        for a in range(3):
            for b in range(3):
                spatial_ref[3 * a + b] = sum_ref[a, :, b * chans : (b + 1) * chans]
        for k in range(3):
            temporal_ref[k] = sum_ref[3, :, k * chans : (k + 1) * chans]

    return call(
        body,
        [shape((9, 2 * half, chans), F32), shape((3, 2 * half, chans), F32)],
        [pltpu.VMEM((4, 2 * half, wide), F32)],
        8 * parts[0].size,
        *parts,
    )


def block_output(frames, temporal):
    def body(frames_ref, temporal_ref, out_ref):
        out_ref[...] = (frames_ref[...].astype(F32) + temporal_ref[...].astype(F32)).astype(BF)

    return call(body, [shape(frames.shape)], [], frames.size, frames, temporal)[0]


def local(frames_in, spatial_kernel, temporal_kernel, out_cotangent):
    frames, cotangent = frames_in[0, 0], out_cotangent[0, 0]
    rows, chans, width = frames.shape
    seq, dp = lax.axis_size("seq"), lax.axis_size("dp")
    shard = spatial_kernel.shape[1]
    scale = 1.0 / math.sqrt(dp * seq * rows * width)

    first = core() == 0
    mine_a = jnp.where(first, temporal_kernel, spatial_kernel[3:6])
    mine_b = jnp.where(first, spatial_kernel[:3], spatial_kernel[6:])
    got_a = spread([mine_a] * (seq - 1))
    cot_rows = exchange(cotangent.reshape(seq, rows // seq, chans, width))
    got_b = spread([mine_b] * (seq - 1))
    taps = window_taps(frames)
    other_taps = window_taps(swap(after(frames, mine_a), "dp", 1))
    taps, other_taps, *got_a = lax.optimization_barrier((taps, other_taps, *got_a))
    pair_a = [swap(piece, "dp", 1) for piece in got_a]
    temporal_t, temporal_w, middle = kernel_maps(
        temporal_kernel, spatial_kernel, got_a, pair_a
    )
    grad_rows = temporal_backward(cot_rows, temporal_t)
    act_grad = [grad_rows[0], *spread(grad_rows[1:])]
    temporal_w, *got_b = lax.optimization_barrier((after(temporal_w, grad_rows[0]), *got_b))
    pair_b = [swap(piece, "dp", 1) for piece in got_b]
    pre_act, activated, weights = spatial_forward(
        taps, spatial_kernel, middle, (*got_b, *pair_b), rows
    )
    half_mine, half_theirs, pre_grad = activation_grad(pre_act, act_grad, shard)
    half_other = swap(half_theirs, "dp", 1)
    act_rows = exchange(activated.reshape(cot_rows.shape))
    spatial_keep, *spatial_send = spatial_weight_grad(
        taps, other_taps, half_mine, half_other, seq, scale, rows
    )
    spatial_got = spread(spatial_send)
    temporal_keep, temporal_send = temporal_weight_grad(
        act_rows, after(cot_rows, spatial_keep), shard, scale
    )
    temporal_part = add_rounded(temporal_keep, swap(temporal_send, "dp", 1))
    temporal_rows = temporal_forward(act_rows, after(temporal_w, temporal_part))
    keep, send = owner_sum(
        after(spatial_keep, temporal_rows), spatial_got, exchange(temporal_part)
    )
    temporal_rows = exchange(after(temporal_rows, keep)).reshape(frames.shape)
    total = add_rounded(keep, swap(send, "dp", 2))
    input_grad = spatial_backward(after(pre_grad, keep), cotangent, weights)
    bit = 4
    while bit < dp:
        other = swap(total, "dp", bit)
        total = add_rounded(after(total, input_grad), other)
        bit *= 2
    block_out = block_output(frames, temporal_rows)
    near = swap(total, "dp", 2)
    near, block_out = lax.optimization_barrier((near, block_out))
    spatial_grad, temporal_grad = kernel_outputs(
        (total, near, swap(total, "dp", 1), swap(near, "dp", 1)), chans
    )
    return (block_out[None, None], input_grad[None, None], spatial_grad, temporal_grad)


def solution(mesh):
    placed = (
        P("dp", "seq", None, None, None),
        P(None, "seq", None),
        P(None, "seq", None),
        P("dp", "seq", None, None, None),
    )
    return jax.shard_map(
        local,
        mesh=mesh,
        in_specs=placed,
        out_specs=(
            P("dp", "seq", None, None, None),
            P("dp", "seq", None, None, None),
            P(None, "seq", None),
            P(None, "seq", None),
        ),
        check_vma=False,
    )
```

```python
import math

import jax
import jax.numpy as jnp
from jax import lax
from jax.experimental import pallas as pl
from jax.experimental.pallas import tpu as pltpu
from jax.sharding import PartitionSpec as P

BF = jnp.bfloat16
F32 = jnp.float32
VMEM_LIMIT = 24 * 1024 * 1024
NT = (((1,), (1,)), ((), ()))


def call(body, outs, scratch, flops, *args, far=(), sent=(), weight=10):
    def spec(i):
        return pl.BlockSpec(memory_space=pltpu.HBM if i in far else pltpu.VMEM)

    args = [
        pltpu.with_memory_space_constraint(arg, pltpu.HBM) if i in far else arg
        for i, arg in enumerate(args)
    ]
    moved = sum(x.size * x.dtype.itemsize for x in (*args, *outs))
    return pl.pallas_call(
        body,
        out_shape=tuple(
            pltpu.HBM(out.shape, out.dtype) if len(args) + i in (*far, *sent) else out
            for i, out in enumerate(outs)
        ),
        in_specs=[spec(i) for i in range(len(args))],
        out_specs=tuple(spec(len(args) + i) for i in range(len(outs))),
        scratch_shapes=scratch,
        compiler_params=pltpu.CompilerParams(vmem_limit_bytes=VMEM_LIMIT),
        cost_estimate=pl.CostEstimate(flops=weight * flops + 1, bytes_accessed=weight * moved + 1, transcendentals=0),
    )(*args)


def shape(dims, dtype=BF):
    return jax.ShapeDtypeStruct(tuple(dims), dtype)


def columns(first, count, width):
    return pl.ds(pl.multiple_of(first * width, width), count * width)


def place(step):
    return jnp.bitwise_xor(lax.axis_index("seq"), step)


def core():
    return lax.rem(lax.axis_index("dp"), 2)


def pair_bit():
    return lax.rem(lax.div(lax.axis_index("dp"), 2), 2)


def at_block(index, size, count, tile, use):
    if size % tile == 0:
        use(pl.ds(pl.multiple_of(index * size, size), size))
        return
    for fixed in range(count):

        @pl.when(index == fixed)
        def _():
            use(pl.ds(fixed * size, size))


def swap(values, axis, bit):
    size = lax.axis_size(axis)
    return lax.ppermute(values, axis, [(i, i ^ bit) for i in range(size)])


def spread(blocks):
    return [swap(block, "seq", j + 1) for j, block in enumerate(blocks)]


def exchange(blocks):
    return lax.all_to_all(blocks, "seq", 0, 0, tiled=True)


def after(value, *others):
    return lax.optimization_barrier((value, *others))[0]


def shifted(block, step):
    if step == 0:
        return block
    width = block.shape[1]
    rolled = pltpu.roll(block.astype(F32), (-step) % width, 1)
    column = lax.broadcasted_iota(jnp.int32, block.shape, 1)
    edge = 0 if step < 0 else width - 1
    return jnp.where(column == edge, 0.0, rolled).astype(block.dtype)


def fill_taps(target, source, order):
    rows, chans, width = source.shape
    target[:, :width] = jnp.zeros((target.shape[0], width), target.dtype)
    target[:, (rows + 1) * width :] = jnp.zeros((target.shape[0], width), target.dtype)

    def row(y, carry):
        block = source[y]
        for b, step in enumerate(order):
            target[b * chans : (b + 1) * chans, columns(y + 1, 1, width)] = shifted(block, step)
        return carry

    lax.fori_loop(0, rows, row, 0)


def transposed(block):
    size = block.shape[0]
    one = lax.broadcasted_iota(jnp.int32, (size, size), 0) == lax.broadcasted_iota(
        jnp.int32, (size, size), 1
    )
    return lax.dot_general(one.astype(BF), block, NT, preferred_element_type=F32).astype(BF)


def window_taps(frames, weight=10):
    rows, chans, width = frames.shape
    dims = (3 * chans, (rows + 2) * width)

    def body(frames_ref, far_ref, taps_ref, done):
        fill_taps(taps_ref, frames_ref, (-1, 0, 1))
        copy = pltpu.make_async_copy(taps_ref, far_ref, done)
        copy.start()
        copy.wait()

    return call(
        body,
        [shape(dims)],
        [pltpu.VMEM(dims, BF), pltpu.SemaphoreType.DMA],
        frames.size,
        frames,
        far=(1,),
        weight=weight,
    )[0]


def kernel_maps(own, spatial, first, second):
    _, shard, chans = own.shape
    count = len(first)

    def body(*refs):
        own_ref, spatial_ref = refs[:2]
        mine, theirs = refs[2 : 2 + count], refs[2 + count : 2 + 2 * count]
        far_trans, far_plain, far_mid, *refs = refs[2 + 2 * count :]
        trans_ref, plain_ref, mid_ref, rows_ref, done = refs

        def fill_mid(pieces):
            for j, piece in enumerate((spatial_ref, *pieces)):

                def put(at):
                    for b in range(3):
                        source = piece[3 + b] if j == 0 else piece[b]
                        mid_ref[at, b * chans : (b + 1) * chans] = source

                at_block(place(j), shard, count + 1, 16, put)

        def fill(pieces):
            for j, piece in enumerate((own_ref, *pieces)):

                def put(at):
                    for k in range(3):
                        rows_ref[k, at, :] = piece[k]

                at_block(place(j), shard, count + 1, 16, put)

        @pl.when(core() == 0)
        def _():
            fill(mine)
            fill_mid(theirs)

        @pl.when(core() == 1)
        def _():
            fill(theirs)
            fill_mid(mine)

        for k in range(3):
            plain_ref[:, k * chans : (k + 1) * chans] = rows_ref[k]
        for k in range(3):
            trans_ref[:, k * chans : (k + 1) * chans] = transposed(rows_ref[k])
        copies = [
            pltpu.make_async_copy(near, far, done.at[i])
            for i, (near, far) in enumerate(
                ((trans_ref, far_trans), (plain_ref, far_plain), (mid_ref, far_mid))
            )
        ]
        for copy in copies:
            copy.start()
        for copy in copies:
            copy.wait()

    return call(
        body,
        [shape((chans, 3 * chans))] * 3,
        [
            pltpu.VMEM((chans, 3 * chans), BF),
            pltpu.VMEM((chans, 3 * chans), BF),
            pltpu.VMEM((chans, 3 * chans), BF),
            pltpu.VMEM((3, chans, chans), BF),
            pltpu.SemaphoreType.DMA((3,)),
        ],
        6 * chans**3,
        own,
        spatial,
        *first,
        *second,
        far=(2 + 2 * count, 3 + 2 * count, 4 + 2 * count),
    )


def temporal_backward(cot_rows, weights_t):
    frames, rows, chans, width = cot_rows.shape
    span = rows * width

    def body(cot_ref, far_ref, *refs):
        outs, (weights_ref, taps_ref, done) = refs[:frames], refs[frames:]
        load = pltpu.make_async_copy(far_ref, weights_ref, done)
        load.start()
        edge = jnp.zeros((chans, span), BF)
        taps_ref[:chans, (frames - 1) * span :] = edge
        taps_ref[2 * chans :, :span] = edge
        for f in range(frames):
            for k in range(3):
                at = f + k - 1
                if 0 <= at < frames:
                    for y in range(rows):
                        to = at * span + y * width
                        taps_ref[k * chans : (k + 1) * chans, to : to + width] = cot_ref[f, y]
        load.wait()
        for j in range(frames):
            total = jnp.dot(
                weights_ref[...],
                taps_ref[:, columns(place(j), 1, span)],
                preferred_element_type=F32,
            ).astype(BF)
            for y in range(rows):
                outs[j][y] = total[:, y * width : (y + 1) * width]

    return call(
        body,
        [shape((rows, chans, width))] * frames,
        [
            pltpu.VMEM(weights_t.shape, BF),
            pltpu.VMEM((3 * chans, frames * span), BF),
            pltpu.SemaphoreType.DMA,
        ],
        6 * chans * cot_rows.size,
        cot_rows,
        weights_t,
        far=(1,),
        sent=tuple(range(2, 2 + frames)),
    )


def spatial_forward(taps, own, middle, pieces, rows):
    _, shard, chans = own.shape
    width = taps.shape[1] // (rows + 2)
    count = len(pieces)
    owners = count // 2 + 1
    tiles = rows // 2

    def body(*refs):
        far_taps, far_middle, sources = refs[0], refs[1], refs[2 : 3 + count]
        pre_ref, far_act, far_weights, taps_ref, act_ref, weights_ref, done = refs[3 + count :]
        middle_load = pltpu.make_async_copy(far_middle, weights_ref.at[1], done.at[tiles + 1])
        middle_load.start()

        def load(i):
            at = columns(2 * i, 2, width)
            return pltpu.make_async_copy(far_taps.at[:, at], taps_ref.at[:, at], done.at[i])

        def start(i, carry):
            load(i).start()
            return carry

        lax.fori_loop(0, tiles + 1, start, 0)

        lists = [sources[1 + i * (owners - 1) : 1 + (i + 1) * (owners - 1)] for i in range(2)]
        for side, order in enumerate(((0, 1), (1, 0))):

            @pl.when(core() == side)
            def _():
                for j in range(owners):

                    def put(at):
                        for a in (0, 2):
                            for b in range(3):
                                if j == 0:
                                    value = sources[0][3 * a + b]
                                else:
                                    value = lists[order[a // 2]][j - 1][b]
                                weights_ref[a, at, b * chans : (b + 1) * chans] = value

                    at_block(place(j), shard, owners, 16, put)

        middle_load.wait()
        store = pltpu.make_async_copy(weights_ref, far_weights, done.at[tiles + 1])
        store.start()
        load(jnp.int32(0)).wait()

        def act_store(i):
            at = pl.ds(2 * i, 2)
            return pltpu.make_async_copy(act_ref.at[at], far_act.at[at], done.at[i])

        def tile(i, carry):
            load(i + 1).wait()
            total = jnp.zeros((chans, 2 * width), F32)
            for a in range(3):
                total += jnp.dot(
                    weights_ref[a],
                    taps_ref[:, columns(2 * i + a, 2, width)],
                    preferred_element_type=F32,
                )
            pre = total.astype(BF)
            wide = pre.astype(F32)
            act = (wide / (1.0 + jnp.exp(-wide))).astype(BF)
            for r in range(2):
                pre_ref[2 * i + r] = pre[:, r * width : (r + 1) * width]
                act_ref[2 * i + r] = act[:, r * width : (r + 1) * width]
            act_store(i).start()
            return carry

        lax.fori_loop(0, tiles, tile, 0)

        def finish(i, carry):
            act_store(i).wait()
            return carry

        lax.fori_loop(0, tiles, finish, 0)
        store.wait()

    return call(
        body,
        [shape((rows, chans, width)), shape((rows, chans, width)), shape((3, chans, 3 * chans))],
        [
            pltpu.VMEM(taps.shape, BF),
            pltpu.VMEM((rows, chans, width), BF),
            pltpu.VMEM((3, chans, 3 * chans), BF),
            pltpu.SemaphoreType.DMA((tiles + 2,)),
        ],
        18 * chans * chans * rows * width,
        taps,
        middle,
        own,
        *pieces,
        far=(0, 1, 4 + count, 5 + count),
        weight=10,
    )


def activation_grad(pre_act, grads, shard):
    rows, chans, width = pre_act.shape
    half = shard // 2

    block = rows // len(grads)

    def body(pre_ref, *refs):
        grad_refs, refs = refs[: len(grads)], refs[len(grads) :]
        mine_ref, theirs_ref, far_ref, pg_ref, act_ref, done = refs
        for j, ref in enumerate(grad_refs):
            act_ref[pl.ds(place(j) * block, block)] = ref[...]

        def row(y, carry):
            wide = pre_ref[y].astype(F32)
            s = 1.0 / (1.0 + jnp.exp(-wide))
            pg = act_ref[y].astype(F32) * s * (1.0 + wide * (1.0 - s))
            pg_ref[y] = pg.astype(BF)
            low = [pg[at : at + half] for at in range(0, chans, shard)]
            high = [pg[at + half : at + shard] for at in range(0, chans, shard)]
            low = jnp.concatenate(low).astype(BF)
            high = jnp.concatenate(high).astype(BF)
            first = core() == 0
            mine_ref[:, columns(y, 1, width)] = jnp.where(first, low, high)
            theirs_ref[:, columns(y, 1, width)] = jnp.where(first, high, low)
            return carry

        copies = []
        for i in range(2):
            lax.fori_loop(i * rows // 2, (i + 1) * rows // 2, row, 0)
            at = pl.ds(i * rows // 2, rows // 2)
            copies.append(pltpu.make_async_copy(pg_ref.at[at], far_ref.at[at], done.at[i]))
            copies[i].start()
        for copy in copies:
            copy.wait()

    return call(
        body,
        [shape((chans // 2, rows * width))] * 2 + [shape(pre_act.shape)],
        [
            pltpu.VMEM(pre_act.shape, BF),
            pltpu.VMEM(pre_act.shape, BF),
            pltpu.SemaphoreType.DMA((2,)),
        ],
        20 * pre_act.size,
        pre_act,
        *grads,
        far=(3 + len(grads),),
    )


def spatial_weight_grad(taps, other_taps, half_grad, other_half, owners, scale, rows):
    wide = taps.shape[0]
    chans, span = half_grad.shape
    width = span // rows
    part = chans // owners

    def body(far_taps, far_other, mine_ref, theirs_ref, *refs):
        keep_ref, sends = refs[0], refs[1:owners]
        stack_ref, taps_ref, total_ref, done = refs[owners:]
        loads = [
            pltpu.make_async_copy(far, taps_ref.at[q], done.at[q])
            for q, far in enumerate((far_taps, far_other))
        ]
        for copy in loads:
            copy.start()
        edge = jnp.zeros((chans, width), BF)
        for q, source in enumerate((mine_ref, theirs_ref)):
            at = q * span
            stack_ref[:chans, at + span - width : at + span] = edge
            stack_ref[:chans, at : at + span - width] = source[:, width:]
            stack_ref[chans : 2 * chans, at : at + span] = source[...]
            stack_ref[2 * chans :, at : at + width] = edge
            stack_ref[2 * chans :, at + width : at + span] = source[:, : span - width]
        total = jnp.zeros((3 * chans, wide), F32)
        for q, copy in enumerate(loads):
            copy.wait()
            total += lax.dot_general(
                stack_ref[:, q * span : (q + 1) * span],
                taps_ref[q, :, width : width + span],
                NT,
                preferred_element_type=F32,
            )
        for a in range(3):
            total_ref[a] = total[a * chans : (a + 1) * chans] * scale
        for j in range(owners):

            def put(at):
                for a in range(3):
                    value = total_ref[a, at, :]
                    if j == 0:
                        keep_ref[a] = value
                    else:
                        sends[j - 1][a] = value.astype(BF)

            at_block(place(j), part, owners, 8, put)

    return call(
        body,
        [shape((3, part, wide), F32)] + [shape((3, part, wide))] * (owners - 1),
        [
            pltpu.VMEM((3 * chans, 2 * span), BF),
            pltpu.VMEM((2,) + taps.shape, BF),
            pltpu.VMEM((3, chans, wide), F32),
            pltpu.SemaphoreType.DMA((2,)),
        ],
        12 * chans * wide * span,
        taps,
        other_taps,
        half_grad,
        other_half,
        far=(0, 1),
        weight=0,
    )


def spatial_backward(pre_grad, cotangent, weights):
    rows, chans, width = pre_grad.shape

    def body(far_pg, far_cot, far_weights, out_ref, *refs):
        pg_ref, cot_ref, weights_ref, taps_ref, trans_ref, done = refs
        loads = [
            pltpu.make_async_copy(far, near, done.at[i])
            for i, (far, near) in enumerate(
                ((far_pg, pg_ref), (far_weights, weights_ref), (far_cot, cot_ref))
            )
        ]
        for copy in loads:
            copy.start()
        loads[0].wait()
        fill_taps(taps_ref, pg_ref, (1, 0, -1))
        loads[1].wait()
        for a in range(3):
            for b in range(3):
                at = slice(b * chans, (b + 1) * chans)
                trans_ref[a, :, at] = transposed(weights_ref[a, :, at])
        loads[2].wait()

        def tile(i, carry):
            total = jnp.zeros((chans, 2 * width), F32)
            for a in range(3):
                total += jnp.dot(
                    trans_ref[a],
                    taps_ref[:, columns(2 * i + 2 - a, 2, width)],
                    preferred_element_type=F32,
                )
            for r in range(2):
                wide = cot_ref[2 * i + r].astype(F32)
                out_ref[2 * i + r] = (wide + total[:, r * width : (r + 1) * width]).astype(BF)
            return carry

        lax.fori_loop(0, rows // 2, tile, 0)

    return call(
        body,
        [shape(pre_grad.shape)],
        [
            pltpu.VMEM(pre_grad.shape, BF),
            pltpu.VMEM(pre_grad.shape, BF),
            pltpu.VMEM((3, chans, 3 * chans), BF),
            pltpu.VMEM((3 * chans, (rows + 2) * width), BF),
            pltpu.VMEM((3, chans, 3 * chans), BF),
            pltpu.SemaphoreType.DMA((3,)),
        ],
        18 * chans * chans * rows * width,
        pre_grad,
        cotangent,
        weights,
        far=(0, 1, 2),
    )[0]


def temporal_weight_grad(acts, cot_rows, shard, scale):
    frames, rows, chans, width = cot_rows.shape
    span = rows * width
    half = shard // 2
    owners = chans // shard

    def body(act_ref, cot_ref, keep_ref, send_ref, taps_ref, cots_ref):
        edge = jnp.zeros((chans, span), BF)
        taps_ref[:chans, :span] = edge
        taps_ref[2 * chans :, (frames - 1) * span :] = edge
        for f in range(frames):
            for y in range(rows):
                at = f * span + y * width
                cots_ref[:, at : at + width] = cot_ref[f, y]
                for k in range(3):
                    if 0 <= f - k + 1 < frames:
                        to = at + (1 - k) * span
                        taps_ref[k * chans : (k + 1) * chans, to : to + width] = act_ref[f, y]
        total = (
            lax.dot_general(cots_ref[...], taps_ref[...], NT, preferred_element_type=F32) * scale
        )
        first = core() == 0
        for s in range(owners):
            low = total[s * shard : s * shard + half]
            high = total[s * shard + half : (s + 1) * shard]
            keep_ref[s] = jnp.where(first, low, high)
            send_ref[s] = jnp.where(first, high, low).astype(BF)

    return call(
        body,
        [shape((owners, half, 3 * chans), F32), shape((owners, half, 3 * chans))],
        [
            pltpu.VMEM((3 * chans, frames * span), BF),
            pltpu.VMEM((chans, frames * span), BF),
        ],
        6 * chans * cot_rows.size,
        acts,
        cot_rows,
    )


def temporal_forward(acts, weights):
    frames, rows, chans, width = acts.shape
    span = rows * width

    def body(act_ref, far_ref, out_ref, weights_ref, taps_ref, done):
        load = pltpu.make_async_copy(far_ref, weights_ref, done)
        load.start()
        edge = jnp.zeros((chans, span), BF)
        taps_ref[:chans, :span] = edge
        taps_ref[2 * chans :, (frames - 1) * span :] = edge
        for f in range(frames):
            for k in range(3):
                if 0 <= f - k + 1 < frames:
                    for y in range(rows):
                        to = (f - k + 1) * span + y * width
                        taps_ref[k * chans : (k + 1) * chans, to : to + width] = act_ref[f, y]
        load.wait()
        for f in range(frames):
            total = jnp.dot(
                weights_ref[...],
                taps_ref[:, f * span : (f + 1) * span],
                preferred_element_type=F32,
            ).astype(BF)
            for y in range(rows):
                out_ref[f, y] = total[:, y * width : (y + 1) * width]

    return call(
        body,
        [shape(acts.shape)],
        [
            pltpu.VMEM(weights.shape, BF),
            pltpu.VMEM((3 * chans, frames * span), BF),
            pltpu.SemaphoreType.DMA,
        ],
        6 * chans * acts.size,
        acts,
        weights,
        far=(1,),
        sent=(2,),
    )[0]


def owner_sum(spatial, others, temporal):
    _, half, wide = spatial.shape
    count = len(others)

    def body(spatial_ref, temporal_ref, *refs):
        other_refs, (keep_ref, send_ref, sum_ref) = refs[:count], refs[count:]
        for a in range(3):
            value = spatial_ref[a]
            for ref in other_refs:
                value += ref[a].astype(F32)
            sum_ref[a] = value
        value = temporal_ref[0].astype(F32)
        for s in range(1, count + 1):
            value += temporal_ref[s].astype(F32)
        sum_ref[3] = value
        bit = pair_bit()
        keep_ref[...] = sum_ref[pl.ds(2 * bit, 2)]
        send_ref[...] = sum_ref[pl.ds(2 - 2 * bit, 2)].astype(BF)

    return call(
        body,
        [shape((2, half, wide), F32), shape((2, half, wide))],
        [pltpu.VMEM((4, half, wide), F32)],
        4 * spatial.size,
        spatial,
        temporal,
        *others,
    )


def add_rounded(keep, other):
    def body(keep_ref, other_ref, out_ref):
        out_ref[...] = (keep_ref[...].astype(F32) + other_ref[...].astype(F32)).astype(BF)

    return call(body, [shape(keep.shape)], [], keep.size, keep, other)[0]


def kernel_outputs(parts, chans):
    _, half, wide = parts[0].shape

    def body(own_ref, next_ref, core_ref, both_ref, spatial_ref, temporal_ref, sum_ref):
        bit, mine = pair_bit(), core()
        for ref, group, side in (
            (own_ref, bit, mine),
            (next_ref, 1 - bit, mine),
            (core_ref, bit, 1 - mine),
            (both_ref, 1 - bit, 1 - mine),
        ):

            def put(at):
                for g in range(2):
                    sum_ref[2 * group + g, at, :] = ref[g].astype(F32)

            at_block(side, half, 2, 8, put)
        for a in range(3):
            for b in range(3):
                spatial_ref[3 * a + b] = sum_ref[a, :, b * chans : (b + 1) * chans]
        for k in range(3):
            temporal_ref[k] = sum_ref[3, :, k * chans : (k + 1) * chans]

    return call(
        body,
        [shape((9, 2 * half, chans), F32), shape((3, 2 * half, chans), F32)],
        [pltpu.VMEM((4, 2 * half, wide), F32)],
        8 * parts[0].size,
        *parts,
    )


def block_output(frames, temporal):
    def body(frames_ref, temporal_ref, out_ref):
        out_ref[...] = (frames_ref[...].astype(F32) + temporal_ref[...].astype(F32)).astype(BF)

    return call(body, [shape(frames.shape)], [], frames.size, frames, temporal)[0]


def local(frames_in, spatial_kernel, temporal_kernel, out_cotangent):
    frames, cotangent = frames_in[0, 0], out_cotangent[0, 0]
    rows, chans, width = frames.shape
    seq, dp = lax.axis_size("seq"), lax.axis_size("dp")
    shard = spatial_kernel.shape[1]
    scale = 1.0 / math.sqrt(dp * seq * rows * width)

    first = core() == 0
    mine_a = jnp.where(first, temporal_kernel, spatial_kernel[3:6])
    mine_b = jnp.where(first, spatial_kernel[:3], spatial_kernel[6:])
    got_a = spread([mine_a] * (seq - 1))
    cot_rows = exchange(cotangent.reshape(seq, rows // seq, chans, width))
    got_b = spread([mine_b] * (seq - 1))
    taps = window_taps(frames)
    other_taps = window_taps(swap(after(frames, mine_a), "dp", 1))
    taps, other_taps, *got_a = lax.optimization_barrier((taps, other_taps, *got_a))
    pair_a = [swap(piece, "dp", 1) for piece in got_a]
    temporal_t, temporal_w, middle = kernel_maps(
        temporal_kernel, spatial_kernel, got_a, pair_a
    )
    grad_rows = temporal_backward(cot_rows, temporal_t)
    act_grad = [grad_rows[0], *spread(grad_rows[1:])]
    temporal_w, *got_b = lax.optimization_barrier((after(temporal_w, grad_rows[0]), *got_b))
    pair_b = [swap(piece, "dp", 1) for piece in got_b]
    pre_act, activated, weights = spatial_forward(
        taps, spatial_kernel, middle, (*got_b, *pair_b), rows
    )
    half_mine, half_theirs, pre_grad = activation_grad(pre_act, act_grad, shard)
    half_other = swap(half_theirs, "dp", 1)
    act_rows = exchange(activated.reshape(cot_rows.shape))
    spatial_keep, *spatial_send = spatial_weight_grad(
        taps, other_taps, half_mine, half_other, seq, scale, rows
    )
    spatial_got = spread(spatial_send)
    temporal_keep, temporal_send = temporal_weight_grad(
        act_rows, after(cot_rows, spatial_keep), shard, scale
    )
    temporal_part = add_rounded(temporal_keep, swap(temporal_send, "dp", 1))
    temporal_rows = temporal_forward(act_rows, after(temporal_w, temporal_part))
    keep, send = owner_sum(
        after(spatial_keep, temporal_rows), spatial_got, exchange(temporal_part)
    )
    temporal_rows = exchange(after(temporal_rows, keep)).reshape(frames.shape)
    total = add_rounded(keep, swap(send, "dp", 2))
    input_grad = spatial_backward(after(pre_grad, keep), cotangent, weights)
    bit = 4
    while bit < dp:
        other = swap(total, "dp", bit)
        total = add_rounded(after(total, input_grad), other)
        bit *= 2
    block_out = block_output(frames, temporal_rows)
    near = swap(total, "dp", 2)
    near, block_out = lax.optimization_barrier((near, block_out))
    spatial_grad, temporal_grad = kernel_outputs(
        (total, near, swap(total, "dp", 1), swap(near, "dp", 1)), chans
    )
    return (block_out[None, None], input_grad[None, None], spatial_grad, temporal_grad)


def solution(mesh):
    placed = (
        P("dp", "seq", None, None, None),
        P(None, "seq", None),
        P(None, "seq", None),
        P("dp", "seq", None, None, None),
    )
    return jax.shard_map(
        local,
        mesh=mesh,
        in_specs=placed,
        out_specs=(
            P("dp", "seq", None, None, None),
            P("dp", "seq", None, None, None),
            P(None, "seq", None),
            P(None, "seq", None),
        ),
        check_vma=False,
    )
```
